1024 devices in a mesh: gx: 16 (over z), gy: 4 (over x), gz: 16 (over y, core).
Axes of the slice: x: 4, y: 8, z: 16, core: 2. Of those that a mesh axis runs over, the one named last changes fastest.
Arguments:
- sources: float32 [32, 64, 64, 512], P(None, 'gz', 'gx', 'gy'), may hold values from -6 to 6
- labels: int32 [64, 64, 512], P('gz', 'gx', 'gy'), may hold values from 1 to 8
- region_table: float32 [8, 4], replicated, may hold values from 0.5 to 2
- sweep_index: int32 [32], replicated, may hold values from 0 to 31
- sweep_gain: float32 [32, 8], replicated, may hold values from 0.5 to 2
Outputs:
- solution: float32 [32, 64, 64, 512], P(None, 'gz', 'gx', 'gy')
- residual: float32 [32, 64, 64, 512], P(None, 'gz', 'gx', 'gy')
The draws below stay inside these ranges and needn't reach their ends.
All inputs are finite; a program needn't handle non-finite values.
Results may differ from the reference program's by a relative error of at most 0.0003.
Values sent between devices are 32-bit elements; how exact they have to be, the bound alone decides.
No kernel may reach another device: no remote copies, remote signals or barrier semaphores. Data moves between devices by JAX's collectives and lax.ppermute only.
A program may use at most 32 MiB of HBM per device.

```python
import math
import jax
import jax.numpy as jnp
from jax import lax

R = 32
S = 4
NREG = 8
NSWEEP = 32
NZ = 64
NX = 64
NY = 512


def touch_ends(entries, own_key, low, top_value):
    longest = entries.shape.index(max(entries.shape))
    spots = []
    for shift in (0, 1):
        where = [jax.random.randint(jax.random.fold_in(own_key, axis), (), 0, length) for axis, length in enumerate(entries.shape)]
        where[longest] = (where[longest] + shift) % entries.shape[longest]
        spots.append(tuple(where))
    return entries.at[spots[0]].set(low).at[spots[1]].set(top_value)


def level_of(key, extent, split, low, top_value):
    def one(dim, parts):
        heights = jax.random.uniform(jax.random.fold_in(jax.random.fold_in(key, 6), dim), (parts,), jnp.float32, low / len(split), top_value / len(split))
        return jnp.repeat(jnp.exp(heights), extent[dim] // parts).reshape((-1,) + (1,) * (len(extent) - dim - 1))

    level = one(*split[0])
    for cut in split[1:]:
        level = level * one(*cut)
    return level


def scatter_about(stream_key, dims, scale, bound, pieces=(), held_as=jnp.bfloat16):
    values = jax.random.normal(stream_key, dims, jnp.float32) * scale
    if len(pieces) > 0:
        values = level_of(stream_key, dims, pieces, -0.22, 0.18) * values
    return jnp.clip(values, min=-bound, max=bound).astype(held_as)


def setup_inputs(seed: int = 0) -> dict:
    keys = jax.random.split(jax.random.key(seed), 6)
    sources = scatter_about(keys[0], (R, NZ, NX, NY), 1.0, 6.0, ((1, 16), (2, 16), (3, 4)), jnp.float32)
    labels = touch_ends(jax.random.randint(keys[1], (NZ, NX, NY), 1, NREG + 1), jax.random.fold_in(keys[1], 1), 1, NREG).astype(jnp.int32)
    region_table = jnp.clip(jnp.exp(jax.random.uniform(keys[2], (NREG, 4), jnp.float32, math.log(0.5), math.log(2.0))), 0.5, 2.0)
    sweep_index = touch_ends(jax.random.randint(keys[3], (R,), 0, NSWEEP), jax.random.fold_in(keys[3], 1), 0, NSWEEP - 1).astype(jnp.int32)
    sweep_gain = jnp.clip(jnp.exp(jax.random.uniform(keys[4], (NSWEEP, NREG), jnp.float32, math.log(0.5), math.log(2.0))), 0.5, 2.0)
    return {"sources": sources, "labels": labels, "region_table": region_table, "sweep_index": sweep_index, "sweep_gain": sweep_gain}


SIGMA = 8.0
THETA = 8.0

def region_fields(labels, region_table):
    fields = [jnp.zeros(labels.shape, jnp.float32) for column in range(4)]
    for region in range(NREG):
        hit = (labels == region + 1).astype(jnp.float32)
        fields = [fields[column] + hit * region_table[region, column] for column in range(4)]
    return fields

def shifted(padded, dim, offset):
    index = [slice(1, -1)] * 3
    index[dim] = slice(1 + offset, padded.shape[dim] - 1 + offset)
    return padded[tuple(index)]

def face_set(fields):
    faces = []
    for dim in range(3):
        padded = jnp.pad(fields[dim], 1)
        faces.append(0.5 * (fields[dim] + shifted(padded, dim, 1)))
        faces.append(0.5 * (fields[dim] + shifted(padded, dim, -1)))
    diag = fields[3] + faces[0] + faces[1] + faces[2] + faces[3] + faces[4] + faces[5]
    return (faces, diag)

def reference(sources, labels, region_table, sweep_index, sweep_gain):
    fields = region_fields(labels, region_table)
    faces, diag = face_set(fields)
    gain_rows = sweep_gain[sweep_index]

    def make_rhs(pair):
        source, row = pair
        gain = jnp.zeros(labels.shape, jnp.float32)
        for region in range(NREG):
            hit = (labels == region + 1).astype(jnp.float32)
            gain = gain + hit * row[region]
        return source * gain
    rhs = lax.map(make_rhs, (sources, gain_rows))

    def power(field):
        padded = jnp.pad(field, 1)
        beside = faces[0] * shifted(padded, 0, 1) + faces[1] * shifted(padded, 0, -1)
        beside = beside + faces[2] * shifted(padded, 1, 1) + faces[3] * shifted(padded, 1, -1)
        beside = beside + faces[4] * shifted(padded, 2, 1) + faces[5] * shifted(padded, 2, -1)
        image = diag * field - beside
        return (image - SIGMA * field) / THETA
    basis = [rhs]
    for step in range(S):
        basis.append(lax.map(power, basis[-1]))
    flats = [block.reshape(R, -1) for block in basis]
    rows_of = []
    for left in flats:
        rows_of.append([jnp.dot(left.astype(jnp.float32), right.T.astype(jnp.float32), precision=lax.Precision.HIGHEST, preferred_element_type=jnp.float32) for right in flats])
    gram = jnp.block(rows_of)
    width = S * R
    mat = THETA * gram[:width, R:] + SIGMA * gram[:width, :width]
    mat = 0.5 * (mat + mat.T)
    factor = jnp.linalg.cholesky(mat)
    coef = jax.scipy.linalg.cho_solve((factor, True), gram[:width, :R])
    combo = jnp.zeros(((S + 1) * R, R), jnp.float32)
    combo = combo.at[:width].add(SIGMA * coef)
    combo = combo.at[R:].add(THETA * coef)
    solution = jnp.zeros(flats[0].shape, jnp.float32)
    taken = jnp.zeros(flats[0].shape, jnp.float32)
    for index in range(S + 1):
        if index < S:
            solution = solution + jnp.dot(coef[index * R:(index + 1) * R].T.astype(jnp.float32), flats[index].astype(jnp.float32), precision=lax.Precision.HIGHEST, preferred_element_type=jnp.float32)
        taken = taken + jnp.dot(combo[index * R:(index + 1) * R].T.astype(jnp.float32), flats[index].astype(jnp.float32), precision=lax.Precision.HIGHEST, preferred_element_type=jnp.float32)
    residual = flats[0] - taken
    return (solution.reshape(sources.shape), residual.reshape(sources.shape))
```

```python
import jax
import jax.numpy as jnp
from jax import lax
from jax.sharding import PartitionSpec as P

S = 4
NREG = 8


SIGMA = 8.0
THETA = 8.0


def padded_2(block, sides, width):
    for axis, dim in sides:
        count = lax.axis_size(axis)
        forward = [(i, i + 1) for i in range(count - 1)]
        backward = [(target, source) for source, target in forward]
        low = lax.ppermute(
            lax.slice_in_dim(block, block.shape[dim] - width, None, axis=dim), axis, forward
        )
        high = lax.ppermute(lax.slice_in_dim(block, 0, width, axis=dim), axis, backward)
        block = jnp.concatenate([low, block, high], axis=dim)
    return block


def region_fields(labels, region_table):
    fields = [jnp.zeros(labels.shape, jnp.float32) for column in range(4)]
    for region in range(NREG):
        hit = (labels == region + 1).astype(jnp.float32)
        fields = [fields[column] + hit * region_table[region, column] for column in range(4)]
    return fields


def trimmed(array, depth):
    lead = [slice(None)] * (array.ndim - 3)
    return array[tuple(lead + [slice(depth, -depth)] * 3)]


def shifted(padded, dim, offset):
    lead = [slice(None)] * (padded.ndim - 3)
    index = [slice(1, -1)] * 3
    size = padded.shape[padded.ndim - 3 + dim]
    index[dim] = slice(1 + offset, size - 1 + offset)
    return padded[tuple(lead + index)]


def face_set(fields):
    faces = []
    for dim in range(3):
        center = trimmed(fields[dim], 1)
        faces.append(0.5 * (center + shifted(fields[dim], dim, 1)))
        faces.append(0.5 * (center + shifted(fields[dim], dim, -1)))
    diag = trimmed(fields[3], 1) + faces[0] + faces[1] + faces[2] + faces[3] + faces[4] + faces[5]
    return (faces, diag)


def next_power(padded, faces, diag):
    beside = faces[0] * shifted(padded, 0, 1) + faces[1] * shifted(padded, 0, -1)
    beside = beside + faces[2] * shifted(padded, 1, 1) + faces[3] * shifted(padded, 1, -1)
    beside = beside + faces[4] * shifted(padded, 2, 1) + faces[5] * shifted(padded, 2, -1)
    center = trimmed(padded, 1)
    image = diag * center - beside
    return (image - SIGMA * center) / THETA


def total(values):
    parts = lax.axis_size("gz")
    others = lax.axis_size("gx") * lax.axis_size("gy")
    pieces = lax.all_to_all(values.reshape(parts, -1, 128), "gz", 0, 0)
    piece = pieces.sum(0)
    pieces = lax.all_to_all(
        jnp.broadcast_to(piece, (others,) + piece.shape), ("gx", "gy"), 0, 0
    )
    piece = pieces.sum(0)
    return lax.all_to_all(jnp.broadcast_to(piece, (parts,) + piece.shape), "gz", 0, 0)


def body(sources, labels, region_table, sweep_index, sweep_gain):
    count = sources.shape[0]
    gain_rows = sweep_gain[sweep_index]
    regions = jnp.arange(1, NREG + 1, dtype=jnp.int32)
    one_hot = (labels.reshape(1, -1) == regions[:, None]).astype(jnp.float32)
    gain = jnp.dot(
        gain_rows, one_hot, precision=lax.Precision.HIGHEST, preferred_element_type=jnp.float32
    )
    rhs = sources * gain.reshape(sources.shape)
    basis = [rhs]
    near_labels = padded_2(labels, (("gx", 1), ("gy", 2), ("gz", 0)), 1)
    faces, diag = face_set(region_fields(near_labels, region_table))
    current = rhs
    for step in range(S):
        padded = padded_2(current, (("gx", 2), ("gy", 3), ("gz", 1)), 1)
        current = next_power(padded, faces, diag)
        basis.append(current)
    flat = jnp.concatenate([block.reshape(count, -1) for block in basis], 0)
    flats = [block.reshape(count, -1) for block in basis]
    moments = []
    for order in range(2 * S):
        moments.append(
            lax.dot_general(
                flats[order // 2],
                flats[order - order // 2],
                (((1,), (1,)), ((), ())),
                precision=lax.Precision.HIGHEST,
                preferred_element_type=jnp.float32,
            )
        )
    moments = total(jnp.stack(moments)).reshape(2 * S, count, count)
    width = S * count
    sums = THETA * moments[1:] + SIGMA * moments[:-1]
    mat = jnp.concatenate(
        [jnp.concatenate([sums[i + j] for j in range(S)], 1) for i in range(S)], 0
    )
    mat = 0.5 * (mat + mat.T)
    factor = jnp.linalg.cholesky(mat)
    coef = jax.scipy.linalg.cho_solve((factor, True), moments[:S].reshape(width, count))
    combo = jnp.zeros(((S + 1) * count, count), jnp.float32)
    combo = combo.at[:width].add(SIGMA * coef)
    combo = combo.at[count:].add(THETA * coef)
    solution = jnp.dot(
        coef.T, flat[:width], precision=lax.Precision.HIGHEST, preferred_element_type=jnp.float32
    )
    taken = jnp.dot(
        combo.T, flat, precision=lax.Precision.HIGHEST, preferred_element_type=jnp.float32
    )
    residual = flat[:count] - taken
    return (solution.reshape(sources.shape), residual.reshape(sources.shape))


def solution(mesh):
    placed = (P(None, "gz", "gx", "gy"), P("gz", "gx", "gy"), P(), P(), P())
    return jax.shard_map(
        body,
        mesh=mesh,
        in_specs=placed,
        out_specs=(P(None, "gz", "gx", "gy"), P(None, "gz", "gx", "gy")),
        check_vma=False,
    )
```

```python
import functools

import jax
import jax.numpy as jnp
from jax import lax
from jax.experimental import pallas as pl
from jax.experimental.pallas import tpu as pltpu
from jax.sharding import PartitionSpec as P

S = 4
NREG = 8
R = 32
SIDE = 4
CELLS = SIDE * SIDE
LANES = 128
WIDE = SIDE + 2 * S
HALF = 16
EDGE_ROWS = R + 8
KEPT = sum(SIDE + 2 * (S - d) for d in range(1, S + 1))
PLANES = KEPT + 5


SIGMA = 8.0
THETA = 8.0

VMEM = pl.BlockSpec(memory_space=pltpu.VMEM)
SMEM = pl.BlockSpec(memory_space=pltpu.SMEM)


def call(kernel, name, outs, specs, scratch=()):
    return pl.pallas_call(
        kernel,
        name=name,
        out_shape=[jax.ShapeDtypeStruct(shape, jnp.float32) for shape in outs],
        in_specs=specs,
        out_specs=[VMEM] * len(outs),
        scratch_shapes=list(scratch),
        compiler_params=pltpu.CompilerParams(vmem_limit_bytes=40 * 1024 * 1024),
    )


def lane_index(shape):
    return lax.broadcasted_iota(jnp.int32, shape, len(shape) - 1)


def rhs_kernel(index_ref, gain_ref, source_ref, label_ref, block_ref, edge_ref, row_ref):
    for j in range(R):
        row_ref[pl.ds(j, 1), :] = gain_ref[pl.ds(index_ref[j], 1), :]
    rows = row_ref[...]
    columns = [jnp.broadcast_to(rows[:, k : k + 1], (R, LANES)) for k in range(NREG)]
    group = lane_index((R, LANES)) // (2 * S)
    group_row = lane_index((8, LANES)) // (2 * S)
    edge = jnp.zeros((R, LANES), jnp.float32)
    edge_label = jnp.zeros((8, LANES), jnp.float32)
    labels = label_ref[...].astype(jnp.float32)
    for cell in range(CELLS):
        label = jnp.broadcast_to(labels[cell : cell + 1, :], (R, LANES))
        gain = jnp.zeros((R, LANES), jnp.float32)
        for k in range(NREG):
            gain = jnp.where(label == k + 1.0, columns[k], gain)
        rhs = source_ref[pl.ds(cell, R, stride=CELLS), :] * gain
        block_ref[cell] = rhs
        turn = (cell * 2 * S + S) % LANES
        edge = jnp.where(group == cell, pltpu.roll(rhs, turn, 1), edge)
        edge_label = jnp.where(
            group_row == cell, pltpu.roll(label[:8], turn, 1), edge_label
        )
    block_ref[CELLS, 0:CELLS, :] = labels
    block_ref[CELLS, CELLS:R, :] = jnp.zeros((R - CELLS, LANES), jnp.float32)
    edge_ref[0:R, :] = edge
    edge_ref[R:EDGE_ROWS, :] = edge_label


def kept_cells(order):
    return [
        (row, x)
        for d, row in zip(range(1, S + 1), order)
        for x in range(-(S - d), SIDE + S - d)
    ]


def merge_kernel(own_ref, low_ref, high_ref, e0, e1, e2, e3, e4, e5, down_ref, up_ref):
    blocks = (low_ref, own_ref, high_ref)
    for out_ref, order in ((down_ref, (0, 1, 2, 3)), (up_ref, (3, 2, 1, 0))):
        for slot, (row, x) in enumerate(kept_cells(order)):
            out_ref[slot] = blocks[(x + SIDE) // SIDE][row * SIDE + x % SIDE]
    left = lane_index((EDGE_ROWS, LANES)) % (2 * S) < S
    for g, (before, after) in enumerate(((e0, e1), (e2, e3), (e4, e5))):
        edge = jnp.where(left, before[...], after[...])
        labels = blocks[g][CELLS, 0:CELLS, :]
        for out_ref in (down_ref, up_ref):
            out_ref[KEPT + g] = edge[:R]
            if g < 2:
                out_ref[KEPT + 3, g * CELLS : (g + 1) * CELLS, :] = labels
            else:
                out_ref[KEPT + 4, 0:CELLS, :] = labels
            out_ref[KEPT + 4, CELLS + g : CELLS + g + 1, :] = edge[R : R + 1]
    for out_ref in (down_ref, up_ref):
        out_ref[KEPT + 4, CELLS + 3 : R, :] = jnp.zeros((R - CELLS - 3, LANES), jnp.float32)


def coefficients(table_ref, label_ref, cond_ref, coef_ref):
    def conduct(z, carry):
        label = label_ref[z]
        fields = [jnp.zeros((2 * HALF, LANES), jnp.float32) for _ in range(4)]
        for region in range(NREG):
            hit = label == region + 1.0
            fields = [
                jnp.where(hit, table_ref[region, column], fields[column]) for column in range(4)
            ]
        for column in range(4):
            cond_ref[column, z] = fields[column]
        return carry

    lax.fori_loop(0, WIDE, conduct, 0)
    lane = lane_index((2 * HALF, LANES))

    def faces(z, carry):
        inside = label_ref[z] > 0.5
        along_z, along_x, along_y, shunt = (cond_ref[column, z] for column in range(4))
        after = pltpu.roll(along_y, LANES - 1, 1)
        before = pltpu.roll(along_y, 1, 1)
        after = jnp.where(lane == LANES - 1, pltpu.roll(after, HALF, 0), after)
        before = jnp.where(lane == 0, pltpu.roll(before, HALF, 0), before)
        found = [
            0.5 * (along_z + cond_ref[0, z + 1]),
            0.5 * (along_z + cond_ref[0, z - 1]),
            0.5 * (along_x + pltpu.roll(along_x, 2 * HALF - 1, 0)),
            0.5 * (along_x + pltpu.roll(along_x, 1, 0)),
            0.5 * (along_y + after),
            0.5 * (along_y + before),
        ]
        diag = shunt
        for face in found:
            diag = diag + face
        found.append(diag - SIGMA)
        for k, value in enumerate(found):
            coef_ref[k, z] = jnp.where(inside, value * (1.0 / THETA), 0.0)
        return carry

    lax.fori_loop(1, WIDE - 1, faces, 0)


def power_row(source_ref, target_ref, coef_ref, z, xs):
    lane = lane_index((R, LANES))
    first, last = lane == 0, lane == LANES - 1
    for x in xs:
        center = [source_ref[z, x, t] for t in range(2)]
        down = [pltpu.roll(value, 1, 1) for value in center]
        up = [pltpu.roll(value, LANES - 1, 1) for value in center]
        for t in range(2):
            row = t * HALF + x

            def weight(k):
                return jnp.broadcast_to(coef_ref[k, z, row : row + 1, :], (R, LANES))

            after = jnp.where(last, up[1 - t], up[t])
            before = jnp.where(first, down[1 - t], down[t])
            beside = weight(0) * source_ref[z + 1, x, t] + weight(1) * source_ref[z - 1, x, t]
            beside = beside + weight(2) * source_ref[z, x + 1, t]
            beside = beside + weight(3) * source_ref[z, x - 1, t]
            beside = beside + weight(4) * after + weight(5) * before
            target_ref[z, x, t] = weight(6) * center[t] - beside


def power_kernel(
    table_ref,
    own_ref,
    low_ref,
    high_ref,
    mid_ref,
    below_ref,
    above_ref,
    basis_ref,
    moment_ref,
    label_ref,
    cond_ref,
    coef_ref,
    even_ref,
    odd_ref,
):
    blocks = (low_ref, own_ref, high_ref)
    label_ref[...] = jnp.zeros(label_ref.shape, jnp.float32)
    sides = ((0, below_ref), (S, mid_ref), (S + SIDE, above_ref))
    for base, ref in sides:
        for g in range(3):
            for row in range(SIDE):
                labels = (
                    ref[KEPT + 3, g * CELLS + row * SIDE : g * CELLS + (row + 1) * SIDE, :]
                    if g < 2
                    else ref[KEPT + 4, row * SIDE : (row + 1) * SIDE, :]
                )
                label_ref[base + row, g * SIDE : (g + 1) * SIDE, :] = labels
                edge = ref[KEPT + 4, CELLS + g : CELLS + g + 1, :]
                for x in range(SIDE):
                    turn = -((row * SIDE + x) * 2 * S + S) % LANES
                    at = HALF + g * SIDE + x
                    label_ref[base + row, at : at + 1, :] = pltpu.roll(edge, turn, 1)
    coefficients(table_ref, label_ref, cond_ref, coef_ref)

    for row in range(SIDE):
        for x in range(-S, SIDE + S):
            even_ref[S + row, S + x, 0] = blocks[(x + SIDE) // SIDE][row * SIDE + x % SIDE]
    for slot, (row, x) in enumerate(kept_cells((3, 2, 1, 0))):
        even_ref[row, S + x, 0] = below_ref[slot]
    for slot, (row, x) in enumerate(kept_cells((0, 1, 2, 3))):
        even_ref[S + SIDE + row, S + x, 0] = above_ref[slot]
    for base, ref in sides:
        for g in range(3):
            edge = ref[KEPT + g]
            for row in range(SIDE):
                for x in range(SIDE):
                    turn = -((row * SIDE + x) * 2 * S + S) % LANES
                    even_ref[base + row, g * SIDE + x, 1] = pltpu.roll(edge, turn, 1)

    refs = (even_ref, odd_ref)
    flats = []
    for k in range(S + 1):
        now = refs[k % 2]
        cells = []
        for row in range(SIDE):
            for x in range(SIDE):
                value = now[S + row, S + x, 0]
                basis_ref[k, row * SIDE + x] = value
                cells.append(value)
        if k < S:
            later = refs[1 - k % 2]

            def one(z, carry):
                power_row(now, later, coef_ref, z, range(k + 1, WIDE - 1 - k))
                return carry

            lax.fori_loop(k + 1, WIDE - 1 - k, one, 0)
    for k in range(S):
        this = jnp.concatenate([basis_ref[k, cell] for cell in range(CELLS)], 1)
        after = jnp.concatenate([basis_ref[k + 1, cell] for cell in range(CELLS)], 1)
        pair = lax.dot_general(
            this,
            jnp.concatenate([this, after], 0),
            (((1,), (1,)), ((), ())),
            precision=lax.Precision.HIGHEST,
            preferred_element_type=jnp.float32,
        )
        half, at = divmod(2 * k * R, LANES)
        moment_ref[half * R : (half + 1) * R, at : at + 2 * R] = pair


def eliminate(mat, right):
    tiles = [mat[8 * i : 8 * i + 8] for i in range(16)]
    sides = [right[8 * i : 8 * i + 8] for i in range(16)]
    sub = lax.broadcasted_iota(jnp.int32, (8, LANES), 0)
    for k in range(S * R):
        p, s = divmod(k, 8)
        row = jnp.broadcast_to(tiles[p][s : s + 1, :], (8, LANES))
        side = jnp.broadcast_to(sides[p][s : s + 1, :], (8, LANES))
        inverse = 1.0 / jnp.broadcast_to(row[:, k : k + 1], (8, LANES))
        row, side = row * inverse, side * inverse
        for i in range(16):
            column = jnp.broadcast_to(tiles[i][:, k : k + 1], (8, LANES))
            tile, rest = tiles[i] - column * row, sides[i] - column * side
            if i == p:
                tile, rest = jnp.where(sub == s, row, tile), jnp.where(sub == s, side, rest)
            tiles[i], sides[i] = tile, rest
    return jnp.concatenate(sides, 0)


def solve_kernel(moment_ref, basis_ref, solution_ref, residual_ref):
    low, high = moment_ref[0:R, :], moment_ref[R : 2 * R, :]
    lane = lane_index((R, LANES))

    def window(first, second, shift):
        if shift == 0:
            return first
        keep = lane < LANES - shift
        turn = LANES - shift
        return jnp.where(keep, pltpu.roll(first, turn, 1), pltpu.roll(second, turn, 1))

    first = THETA * window(low, high, R) + SIGMA * low
    second = THETA * window(high, high, R) + SIGMA * high
    mat = jnp.concatenate([window(first, second, i * R) for i in range(S)], 0)
    mat = 0.5 * (mat + mat.T)
    right = jnp.concatenate([window(low, high, i * R) for i in range(S)], 0)
    coef = eliminate(mat, right)
    zero = jnp.zeros((R, LANES), jnp.float32)
    here = jnp.concatenate([coef, zero], 0)
    there = jnp.concatenate([zero, coef], 0)
    combo = SIGMA * here + THETA * there
    wide = lane_index(here.shape)
    weights = jnp.where(
        wide < R, here, jnp.where(wide < 2 * R, pltpu.roll(combo, R, 1), 0.0)
    )
    weights = jnp.concatenate([weights, jnp.zeros((96, LANES), jnp.float32)], 0)
    weights = weights.T[: 2 * R, : (S + 1) * R]
    for cell in range(CELLS):
        block = jnp.concatenate([basis_ref[k, cell] for k in range(S + 1)], 0)
        taken = lax.dot_general(
            weights,
            block,
            (((1,), (0,)), ((), ())),
            precision=lax.Precision.HIGHEST,
            preferred_element_type=jnp.float32,
        )
        solution_ref[pl.ds(cell, R, stride=CELLS), :] = taken[:R]
        residual_ref[pl.ds(cell, R, stride=CELLS), :] = basis_ref[0, cell] - taken[R:]


def neighbour(value, axes, offsets):
    sizes = [lax.axis_size(axis) for axis in axes]
    pairs = []
    for at in range(sizes[0] * (sizes[1] if len(sizes) > 1 else 1)):
        place = divmod(at, sizes[1]) if len(sizes) > 1 else (at,)
        to = [p + o for p, o in zip(place, offsets)]
        if all(0 <= t < n for t, n in zip(to, sizes)):
            pairs.append((at, to[0] if len(to) == 1 else to[0] * sizes[1] + to[1]))
    return lax.ppermute(value, axes if len(axes) > 1 else axes[0], pairs)


def total(values):
    parts = lax.axis_size("gz")
    others = lax.axis_size("gx") * lax.axis_size("gy")
    pieces = lax.all_to_all(values.reshape(parts, -1, LANES), "gz", 0, 0)
    piece = pieces.sum(0)
    pieces = lax.all_to_all(
        jnp.broadcast_to(piece, (others,) + piece.shape), ("gx", "gy"), 0, 0
    )
    piece = pieces.sum(0)
    pieces = lax.all_to_all(jnp.broadcast_to(piece, (parts,) + piece.shape), "gz", 0, 0)
    return pieces.reshape(values.shape)


def body(sources, labels, region_table, sweep_index, sweep_gain):
    block, edge = call(
        rhs_kernel,
        "rhs",
        [(CELLS + 1, R, LANES), (EDGE_ROWS, LANES)],
        [SMEM, VMEM, VMEM, VMEM],
        [pltpu.VMEM((R, NREG), jnp.float32)],
    )(sweep_index, sweep_gain, sources.reshape(R * CELLS, LANES), labels.reshape(CELLS, LANES))
    low = neighbour(block, ("gx",), (1,))
    high = neighbour(block, ("gx",), (-1,))
    edges = [
        neighbour(edge, ("gx", "gy"), (dx, dy)) for dx in (1, 0, -1) for dy in (1, -1)
    ]
    down, up = call(
        merge_kernel, "merge", [(PLANES, R, LANES)] * 2, [VMEM] * 9
    )(block, low, high, *edges)
    below = neighbour(up, ("gz",), (1,))
    above = neighbour(down, ("gz",), (-1,))
    basis, moments = call(
        power_kernel,
        "powers",
        [(S + 1, CELLS, R, LANES), (2 * R, LANES)],
        [SMEM] + [VMEM] * 6,
        [
            pltpu.VMEM((WIDE, 2 * HALF, LANES), jnp.float32),
            pltpu.VMEM((4, WIDE, 2 * HALF, LANES), jnp.float32),
            pltpu.VMEM((7, WIDE, 2 * HALF, LANES), jnp.float32),
            pltpu.VMEM((WIDE, WIDE, 2, R, LANES), jnp.float32),
            pltpu.VMEM((WIDE, WIDE, 2, R, LANES), jnp.float32),
        ],
    )(region_table, block, low, high, down, below, above)
    solution, residual = call(
        solve_kernel, "solve", [(R * CELLS, LANES)] * 2, [VMEM] * 2
    )(total(moments), basis)
    return (solution.reshape(sources.shape), residual.reshape(sources.shape))


def solution(mesh):
    placed = (P(None, "gz", "gx", "gy"), P("gz", "gx", "gy"), P(), P(), P())
    return jax.shard_map(
        body,
        mesh=mesh,
        in_specs=placed,
        out_specs=(P(None, "gz", "gx", "gy"), P(None, "gz", "gx", "gy")),
        check_vma=False,
    )
```

```python
import jax
import jax.numpy as jnp
from jax import lax
from jax.experimental import pallas as pl
from jax.experimental.pallas import tpu as pltpu
from jax.sharding import PartitionSpec as P

S = 4
NREG = 8
R = 32
SIDE = 4
CELLS = SIDE * SIDE
LANES = 128
WIDE = SIDE + 2 * S
HALF = 16
EDGE_ROWS = R + 8
KEPT = sum(SIDE + 2 * (S - d) for d in range(1, S + 1))
PLANES = KEPT + 5


SIGMA = 8.0
THETA = 8.0

VMEM = pl.BlockSpec(memory_space=pltpu.VMEM)
SMEM = pl.BlockSpec(memory_space=pltpu.SMEM)
HBM = pl.BlockSpec(memory_space=pltpu.HBM)


def call(kernel, name, outs, specs, scratch=(), mebi=8):
    return pl.pallas_call(
        kernel,
        name=name,
        out_shape=[jax.ShapeDtypeStruct(shape, jnp.float32) for shape in outs],
        in_specs=specs,
        out_specs=[VMEM] * len(outs),
        scratch_shapes=list(scratch),
        compiler_params=pltpu.CompilerParams(vmem_limit_bytes=mebi * 1024 * 1024),
    )


def lane_index(shape):
    return lax.broadcasted_iota(jnp.int32, shape, len(shape) - 1)


def rhs_kernel(
    index_ref, gain_ref, source_hbm, label_hbm, block_ref, edge_ref, source_ref, label_ref, sems
):
    copies = [
        pltpu.make_async_copy(source_hbm, source_ref, sems.at[0]),
        pltpu.make_async_copy(label_hbm, label_ref, sems.at[1]),
    ]
    for copy in copies:
        copy.start()
    sub = lax.broadcasted_iota(jnp.int32, (R, gain_ref.shape[1]), 0)
    point = jnp.zeros(sub.shape, jnp.int32)
    for j in range(R):
        point = jnp.where(sub == j, index_ref[j], point)
    rows = lax.dot_general(
        (point == lane_index(point.shape)).astype(jnp.float32),
        gain_ref[...],
        (((1,), (1,)), ((), ())),
        precision=lax.Precision.HIGHEST,
        preferred_element_type=jnp.float32,
    )
    columns = [jnp.broadcast_to(rows[:, k : k + 1], (R, LANES)) for k in range(NREG)]
    for copy in copies:
        copy.wait()
    group = lane_index((R, LANES)) // (2 * S)
    group_row = lane_index((8, LANES)) // (2 * S)
    edge = jnp.zeros((R, LANES), jnp.float32)
    edge_label = jnp.zeros((8, LANES), jnp.float32)
    labels = label_ref[...].astype(jnp.float32)
    for cell in range(CELLS):
        label = jnp.broadcast_to(labels[cell : cell + 1, :], (R, LANES))
        gain = jnp.zeros((R, LANES), jnp.float32)
        for k in range(NREG):
            gain = jnp.where(label == k + 1.0, columns[k], gain)
        rhs = source_ref[pl.ds(cell, R, stride=CELLS), :] * gain
        block_ref[cell] = rhs
        turn = (cell * 2 * S + S) % LANES
        edge = jnp.where(group == cell, pltpu.roll(rhs, turn, 1), edge)
        edge_label = jnp.where(
            group_row == cell, pltpu.roll(label[:8], turn, 1), edge_label
        )
    block_ref[CELLS, 0:CELLS, :] = labels
    block_ref[CELLS, CELLS:R, :] = jnp.zeros((R - CELLS, LANES), jnp.float32)
    edge_ref[0:R, :] = edge
    edge_ref[R:EDGE_ROWS, :] = edge_label


def join_kernel(block_ref, before_ref, after_ref, out_ref):
    left = lane_index((EDGE_ROWS, LANES)) % (2 * S) < S
    edge = jnp.where(left, before_ref[...], after_ref[...])
    out_ref[0 : CELLS + 1] = block_ref[...]
    out_ref[CELLS, CELLS : CELLS + 1, :] = edge[R : R + 1]
    out_ref[CELLS + 1] = edge[:R]


def kept_cells(order):
    return [
        (row, x)
        for d, row in zip(range(1, S + 1), order)
        for x in range(-(S - d), SIDE + S - d)
    ]


def merge_kernel(own_ref, low_ref, high_ref, down_ref, up_ref):
    blocks = (low_ref, own_ref, high_ref)
    for out_ref, order in ((down_ref, (0, 1, 2, 3)), (up_ref, (3, 2, 1, 0))):
        for slot, (row, x) in enumerate(kept_cells(order)):
            out_ref[slot] = blocks[(x + SIDE) // SIDE][row * SIDE + x % SIDE]
        for g in range(3):
            out_ref[KEPT + g] = blocks[g][CELLS + 1]
            labels = blocks[g][CELLS, 0:CELLS, :]
            if g < 2:
                out_ref[KEPT + 3, g * CELLS : (g + 1) * CELLS, :] = labels
            else:
                out_ref[KEPT + 4, 0:CELLS, :] = labels
            edge = blocks[g][CELLS, CELLS : CELLS + 1, :]
            out_ref[KEPT + 4, CELLS + g : CELLS + g + 1, :] = edge
        out_ref[KEPT + 4, CELLS + 3 : R, :] = jnp.zeros((R - CELLS - 3, LANES), jnp.float32)


def coefficients(table_ref, label_ref, cond_ref, coef_ref):
    def conduct(z, carry):
        label = label_ref[z]
        fields = [jnp.zeros((2 * HALF, LANES), jnp.float32) for _ in range(4)]
        for region in range(NREG):
            hit = label == region + 1.0
            fields = [
                jnp.where(hit, table_ref[column, region], fields[column]) for column in range(4)
            ]
        for column in range(4):
            cond_ref[column, z] = fields[column]
        return carry

    lax.fori_loop(0, WIDE, conduct, 0)
    lane = lane_index((2 * HALF, LANES))

    def faces(z, carry):
        inside = label_ref[z] > 0.5
        along_z, along_x, along_y, shunt = (cond_ref[column, z] for column in range(4))
        after = pltpu.roll(along_y, LANES - 1, 1)
        before = pltpu.roll(along_y, 1, 1)
        after = jnp.where(lane == LANES - 1, pltpu.roll(after, HALF, 0), after)
        before = jnp.where(lane == 0, pltpu.roll(before, HALF, 0), before)
        found = [
            0.5 * (along_z + cond_ref[0, z + 1]),
            0.5 * (along_z + cond_ref[0, z - 1]),
            0.5 * (along_x + pltpu.roll(along_x, 2 * HALF - 1, 0)),
            0.5 * (along_x + pltpu.roll(along_x, 1, 0)),
            0.5 * (along_y + after),
            0.5 * (along_y + before),
        ]
        diag = shunt
        for face in found:
            diag = diag + face
        found.append(diag - SIGMA)
        for k, value in enumerate(found):
            coef_ref[k, z] = jnp.where(inside, value * (1.0 / THETA), 0.0)
        return carry

    lax.fori_loop(1, WIDE - 1, faces, 0)


def power_row(source_ref, target_ref, coef_ref, z, xs):
    lane = lane_index((R, LANES))
    first, last = lane == 0, lane == LANES - 1
    for x in xs:
        center = [source_ref[z, x, t] for t in range(2)]
        down = [pltpu.roll(value, 1, 1) for value in center]
        up = [pltpu.roll(value, LANES - 1, 1) for value in center]
        for t in range(2):
            row = t * HALF + x

            def weight(k):
                return jnp.broadcast_to(coef_ref[k, z, row : row + 1, :], (R, LANES))

            after = jnp.where(last, up[1 - t], up[t])
            before = jnp.where(first, down[1 - t], down[t])
            beside = weight(0) * source_ref[z + 1, x, t] + weight(1) * source_ref[z - 1, x, t]
            beside = beside + weight(2) * source_ref[z, x + 1, t]
            beside = beside + weight(3) * source_ref[z, x - 1, t]
            beside = beside + weight(4) * after + weight(5) * before
            target_ref[z, x, t] = weight(6) * center[t] - beside


def power_kernel(
    table_ref,
    own_ref,
    low_ref,
    high_ref,
    mid_ref,
    below_ref,
    above_ref,
    basis_ref,
    moment_ref,
    label_ref,
    cond_ref,
    coef_ref,
    even_ref,
    odd_ref,
):
    blocks = (low_ref, own_ref, high_ref)
    label_ref[...] = jnp.zeros(label_ref.shape, jnp.float32)
    sides = ((0, below_ref), (S, mid_ref), (S + SIDE, above_ref))
    for base, ref in sides:
        for g in range(3):
            for row in range(SIDE):
                labels = (
                    ref[KEPT + 3, g * CELLS + row * SIDE : g * CELLS + (row + 1) * SIDE, :]
                    if g < 2
                    else ref[KEPT + 4, row * SIDE : (row + 1) * SIDE, :]
                )
                label_ref[base + row, g * SIDE : (g + 1) * SIDE, :] = labels
                edge = ref[KEPT + 4, CELLS + g : CELLS + g + 1, :]
                for x in range(SIDE):
                    turn = -((row * SIDE + x) * 2 * S + S) % LANES
                    at = HALF + g * SIDE + x
                    label_ref[base + row, at : at + 1, :] = pltpu.roll(edge, turn, 1)
    coefficients(table_ref, label_ref, cond_ref, coef_ref)

    for row in range(SIDE):
        for x in range(-S, SIDE + S):
            even_ref[S + row, S + x, 0] = blocks[(x + SIDE) // SIDE][row * SIDE + x % SIDE]
    for slot, (row, x) in enumerate(kept_cells((3, 2, 1, 0))):
        even_ref[row, S + x, 0] = below_ref[slot]
    for slot, (row, x) in enumerate(kept_cells((0, 1, 2, 3))):
        even_ref[S + SIDE + row, S + x, 0] = above_ref[slot]
    for base, ref in sides:
        for g in range(3):
            edge = ref[KEPT + g]
            for row in range(SIDE):
                for x in range(SIDE):
                    turn = -((row * SIDE + x) * 2 * S + S) % LANES
                    even_ref[base + row, g * SIDE + x, 1] = pltpu.roll(edge, turn, 1)

    refs = (even_ref, odd_ref)
    flats = []
    for k in range(S + 1):
        now = refs[k % 2]
        cells = []
        for row in range(SIDE):
            for x in range(SIDE):
                value = now[S + row, S + x, 0]
                basis_ref[k, row * SIDE + x] = value
                cells.append(value)
        if k < S:
            later = refs[1 - k % 2]

            def one(z, carry):
                power_row(now, later, coef_ref, z, range(k + 1, WIDE - 1 - k))
                return carry

            lax.fori_loop(k + 1, WIDE - 1 - k, one, 0)
    for k in range(S):
        this = jnp.concatenate([basis_ref[k, cell] for cell in range(CELLS)], 1)
        after = jnp.concatenate([basis_ref[k + 1, cell] for cell in range(CELLS)], 1)
        pair = lax.dot_general(
            this,
            jnp.concatenate([this, after], 0),
            (((1,), (1,)), ((), ())),
            precision=lax.Precision.HIGHEST,
            preferred_element_type=jnp.float32,
        )
        half, at = divmod(2 * k * R, LANES)
        moment_ref[half * R : (half + 1) * R, at : at + 2 * R] = pair


def eliminate(mat, right):
    tiles = [mat[8 * i : 8 * i + 8] for i in range(16)]
    sides = [right[8 * i : 8 * i + 8] for i in range(16)]
    sub = lax.broadcasted_iota(jnp.int32, (8, LANES), 0)

    def spread(row):
        return jnp.broadcast_to(row, (8, LANES))

    for k in range(0, S * R, 4):
        p, s = divmod(k, 8)
        a = [spread(tiles[p][s + i : s + i + 1, :]) for i in range(4)]
        b = [spread(sides[p][s + i : s + i + 1, :]) for i in range(4)]
        e = {(i, j): spread(a[i][:, k + j : k + j + 1]) for i in range(4) for j in range(i, 4)}
        inv = 1.0 / (e[0, 0] * e[1, 1] - e[0, 1] * e[0, 1])
        q00, q01, q11 = e[1, 1] * inv, -e[0, 1] * inv, e[0, 0] * inv
        w = [[q00 * e[0, j] + q01 * e[1, j] for j in (2, 3)], [q01 * e[0, j] + q11 * e[1, j] for j in (2, 3)]]
        c00 = e[2, 2] - (e[0, 2] * w[0][0] + e[1, 2] * w[1][0])
        c01 = e[2, 3] - (e[0, 2] * w[0][1] + e[1, 2] * w[1][1])
        c11 = e[3, 3] - (e[0, 3] * w[0][1] + e[1, 3] * w[1][1])
        inv = 1.0 / (c00 * c11 - c01 * c01)
        d00, d01, d11 = c11 * inv, -c01 * inv, c00 * inv

        def solve(r):
            y0 = r[2] - (w[0][0] * r[0] + w[1][0] * r[1])
            y1 = r[3] - (w[0][1] * r[0] + w[1][1] * r[1])
            x2 = d00 * y0 + d01 * y1
            x3 = d01 * y0 + d11 * y1
            x0 = (q00 * r[0] + q01 * r[1]) - (w[0][0] * x2 + w[0][1] * x3)
            x1 = (q01 * r[0] + q11 * r[1]) - (w[1][0] * x2 + w[1][1] * x3)
            return [x0, x1, x2, x3]

        a, b = solve(a), solve(b)
        for i in range(16):
            col = [spread(tiles[i][:, k + j : k + j + 1]) for j in range(4)]
            tile = tiles[i] - ((col[0] * a[0] + col[1] * a[1]) + (col[2] * a[2] + col[3] * a[3]))
            rest = sides[i] - ((col[0] * b[0] + col[1] * b[1]) + (col[2] * b[2] + col[3] * b[3]))
            if i == p:
                for j in range(4):
                    tile = jnp.where(sub == s + j, a[j], tile)
                    rest = jnp.where(sub == s + j, b[j], rest)
            tiles[i], sides[i] = tile, rest
    return jnp.concatenate(sides, 0)


def solve_kernel(moment_ref, basis_ref, solution_ref, residual_ref):
    low, high = moment_ref[0:R, :], moment_ref[R : 2 * R, :]
    lane = lane_index((R, LANES))

    def window(first, second, shift):
        if shift == 0:
            return first
        keep = lane < LANES - shift
        turn = LANES - shift
        return jnp.where(keep, pltpu.roll(first, turn, 1), pltpu.roll(second, turn, 1))

    first = THETA * window(low, high, R) + SIGMA * low
    second = THETA * window(high, high, R) + SIGMA * high
    mat = jnp.concatenate([window(first, second, i * R) for i in range(S)], 0)
    mat = 0.5 * (mat + mat.T)
    right = jnp.concatenate([window(low, high, i * R) for i in range(S)], 0)
    coef = eliminate(mat, right)
    zero = jnp.zeros((R, LANES), jnp.float32)
    here = jnp.concatenate([coef, zero], 0)
    there = jnp.concatenate([zero, coef], 0)
    combo = SIGMA * here + THETA * there
    wide = lane_index(here.shape)
    weights = jnp.where(
        wide < R, here, jnp.where(wide < 2 * R, pltpu.roll(combo, R, 1), 0.0)
    )
    weights = jnp.concatenate([weights, jnp.zeros((96, LANES), jnp.float32)], 0)
    weights = weights.T[: 2 * R, : (S + 1) * R]
    for cell in range(CELLS):
        block = jnp.concatenate([basis_ref[k, cell] for k in range(S + 1)], 0)
        taken = lax.dot_general(
            weights,
            block,
            (((1,), (0,)), ((), ())),
            precision=lax.Precision.HIGHEST,
            preferred_element_type=jnp.float32,
        )
        solution_ref[pl.ds(cell, R, stride=CELLS), :] = taken[:R]
        residual_ref[pl.ds(cell, R, stride=CELLS), :] = basis_ref[0, cell] - taken[R:]


def neighbour(value, axis, offset):
    count = lax.axis_size(axis)
    pairs = [(at, at + offset) for at in range(count) if 0 <= at + offset < count]
    return lax.ppermute(value, axis, pairs)


def total(values):
    parts = lax.axis_size("gz")
    others = lax.axis_size("gx") * lax.axis_size("gy")
    pieces = lax.all_to_all(values.reshape(parts, -1, LANES), "gz", 0, 0)
    piece = pieces.sum(0)
    pieces = lax.all_to_all(
        jnp.broadcast_to(piece, (others,) + piece.shape), ("gx", "gy"), 0, 0
    )
    piece = pieces.sum(0)
    pieces = lax.all_to_all(jnp.broadcast_to(piece, (parts,) + piece.shape), "gz", 0, 0)
    return pieces.reshape(values.shape)


def body(sources, labels, region_table, sweep_index, sweep_gain):
    block, edge = call(
        rhs_kernel,
        "rhs",
        [(CELLS + 1, R, LANES), (EDGE_ROWS, LANES)],
        [SMEM, VMEM, HBM, HBM],
        [
            pltpu.VMEM((R * CELLS, LANES), jnp.float32),
            pltpu.VMEM((CELLS, LANES), jnp.int32),
            pltpu.SemaphoreType.DMA((2,)),
        ],
    )(sweep_index, sweep_gain.T, sources.reshape(R * CELLS, LANES), labels.reshape(CELLS, LANES))
    before, after = neighbour(edge, "gy", 1), neighbour(edge, "gy", -1)
    block = call(join_kernel, "join", [(CELLS + 2, R, LANES)], [VMEM] * 3)(block, before, after)[0]
    low, high = neighbour(block, "gx", 1), neighbour(block, "gx", -1)
    down, up = call(merge_kernel, "merge", [(PLANES, R, LANES)] * 2, [VMEM] * 3)(
        block, low, high
    )
    below, above = neighbour(up, "gz", 1), neighbour(down, "gz", -1)
    basis, moments = call(
        power_kernel,
        "powers",
        [(S + 1, CELLS, R, LANES), (2 * R, LANES)],
        [SMEM] + [VMEM] * 6,
        [
            pltpu.VMEM((WIDE, 2 * HALF, LANES), jnp.float32),
            pltpu.VMEM((4, WIDE, 2 * HALF, LANES), jnp.float32),
            pltpu.VMEM((7, WIDE, 2 * HALF, LANES), jnp.float32),
            pltpu.VMEM((WIDE, WIDE, 2, R, LANES), jnp.float32),
            pltpu.VMEM((WIDE, WIDE, 2, R, LANES), jnp.float32),
        ],
            24,
    )(region_table.T, block, low, high, down, below, above)
    solution, residual = call(
        solve_kernel, "solve", [(R * CELLS, LANES)] * 2, [VMEM] * 2
    )(total(moments), basis)
    return (solution.reshape(sources.shape), residual.reshape(sources.shape))


def solution(mesh):
    placed = (P(None, "gz", "gx", "gy"), P("gz", "gx", "gy"), P(), P(), P())
    return jax.shard_map(
        body,
        mesh=mesh,
        in_specs=placed,
        out_specs=(P(None, "gz", "gx", "gy"), P(None, "gz", "gx", "gy")),
        check_vma=False,
    )
```

```python
import jax
import jax.numpy as jnp
from jax import lax
from jax.experimental import pallas as pl
from jax.experimental.pallas import tpu as pltpu
from jax.sharding import PartitionSpec as P

S = 4
NREG = 8
R = 32
SIDE = 4
CELLS = SIDE * SIDE
LANES = 128
WIDE = SIDE + 2 * S
HALF = 16
EDGE_ROWS = R + 8
KEPT = sum(SIDE + 2 * (S - d) for d in range(1, S + 1))
PLANES = KEPT + 5


SIGMA = 8.0
THETA = 8.0

VMEM = pl.BlockSpec(memory_space=pltpu.VMEM)
SMEM = pl.BlockSpec(memory_space=pltpu.SMEM)


def call(kernel, name, outs, specs, scratch=(), mebi=8):
    return pl.pallas_call(
        kernel,
        name=name,
        out_shape=[jax.ShapeDtypeStruct(shape, jnp.float32) for shape in outs],
        in_specs=specs,
        out_specs=[VMEM] * len(outs),
        scratch_shapes=list(scratch),
        compiler_params=pltpu.CompilerParams(vmem_limit_bytes=mebi * 1024 * 1024),
    )


def lane_index(shape):
    return lax.broadcasted_iota(jnp.int32, shape, len(shape) - 1)


def gain_kernel(index_ref, gain_ref, row_ref):
    sub = lax.broadcasted_iota(jnp.int32, (R, gain_ref.shape[1]), 0)
    point = jnp.zeros(sub.shape, jnp.int32)
    for j in range(R):
        point = jnp.where(sub == j, index_ref[j], point)
    row_ref[...] = lax.dot_general(
        (point == lane_index(point.shape)).astype(jnp.float32),
        gain_ref[...],
        (((1,), (1,)), ((), ())),
        precision=lax.Precision.HIGHEST,
        preferred_element_type=jnp.float32,
    )


def rhs_kernel(row_ref, source_ref, label_ref, block_ref, edge_ref):
    rows = row_ref[...]
    columns = [jnp.broadcast_to(rows[:, k : k + 1], (R, LANES)) for k in range(NREG)]
    group = lane_index((R, LANES)) // (2 * S)
    group_row = lane_index((8, LANES)) // (2 * S)
    edge = jnp.zeros((R, LANES), jnp.float32)
    edge_label = jnp.zeros((8, LANES), jnp.float32)
    labels = label_ref[...].astype(jnp.float32)
    for cell in range(CELLS):
        label = jnp.broadcast_to(labels[cell : cell + 1, :], (R, LANES))
        gain = jnp.zeros((R, LANES), jnp.float32)
        for k in range(NREG):
            gain = jnp.where(label == k + 1.0, columns[k], gain)
        rhs = source_ref[pl.ds(cell, R, stride=CELLS), :] * gain
        block_ref[cell] = rhs
        turn = (cell * 2 * S + S) % LANES
        edge = jnp.where(group == cell, pltpu.roll(rhs, turn, 1), edge)
        edge_label = jnp.where(
            group_row == cell, pltpu.roll(label[:8], turn, 1), edge_label
        )
    block_ref[CELLS, 0:CELLS, :] = labels
    block_ref[CELLS, CELLS:R, :] = jnp.zeros((R - CELLS, LANES), jnp.float32)
    edge_ref[0:R, :] = edge
    edge_ref[R:EDGE_ROWS, :] = edge_label


def join_kernel(block_ref, before_ref, after_ref, out_ref):
    left = lane_index((EDGE_ROWS, LANES)) % (2 * S) < S
    edge = jnp.where(left, before_ref[...], after_ref[...])
    out_ref[0 : CELLS + 1] = block_ref[...]
    out_ref[CELLS, CELLS : CELLS + 1, :] = edge[R : R + 1]
    out_ref[CELLS + 1] = edge[:R]


def kept_cells(order):
    return [
        (row, x)
        for d, row in zip(range(1, S + 1), order)
        for x in range(-(S - d), SIDE + S - d)
    ]


def merge_kernel(own_ref, low_ref, high_ref, down_ref, up_ref):
    blocks = (low_ref, own_ref, high_ref)
    for out_ref, order in ((down_ref, (0, 1, 2, 3)), (up_ref, (3, 2, 1, 0))):
        for slot, (row, x) in enumerate(kept_cells(order)):
            out_ref[slot] = blocks[(x + SIDE) // SIDE][row * SIDE + x % SIDE]
        for g in range(3):
            out_ref[KEPT + g] = blocks[g][CELLS + 1]
            labels = blocks[g][CELLS, 0:CELLS, :]
            if g < 2:
                out_ref[KEPT + 3, g * CELLS : (g + 1) * CELLS, :] = labels
            else:
                out_ref[KEPT + 4, 0:CELLS, :] = labels
            edge = blocks[g][CELLS, CELLS : CELLS + 1, :]
            out_ref[KEPT + 4, CELLS + g : CELLS + g + 1, :] = edge
        out_ref[KEPT + 4, CELLS + 3 : R, :] = jnp.zeros((R - CELLS - 3, LANES), jnp.float32)


def coefficients(table_ref, label_ref, cond_ref, coef_ref):
    def conduct(z, carry):
        label = label_ref[z]
        fields = [jnp.zeros((2 * HALF, LANES), jnp.float32) for _ in range(4)]
        for region in range(NREG):
            hit = label == region + 1.0
            fields = [
                jnp.where(hit, table_ref[column, region], fields[column]) for column in range(4)
            ]
        for column in range(4):
            cond_ref[column, z] = fields[column]
        return carry

    lax.fori_loop(0, WIDE, conduct, 0)
    lane = lane_index((2 * HALF, LANES))

    def faces(z, carry):
        inside = label_ref[z] > 0.5
        along_z, along_x, along_y, shunt = (cond_ref[column, z] for column in range(4))
        after = pltpu.roll(along_y, LANES - 1, 1)
        before = pltpu.roll(along_y, 1, 1)
        after = jnp.where(lane == LANES - 1, pltpu.roll(after, HALF, 0), after)
        before = jnp.where(lane == 0, pltpu.roll(before, HALF, 0), before)
        found = [
            0.5 * (along_z + cond_ref[0, z + 1]),
            0.5 * (along_z + cond_ref[0, z - 1]),
            0.5 * (along_x + pltpu.roll(along_x, 2 * HALF - 1, 0)),
            0.5 * (along_x + pltpu.roll(along_x, 1, 0)),
            0.5 * (along_y + after),
            0.5 * (along_y + before),
        ]
        diag = shunt
        for face in found:
            diag = diag + face
        found.append(diag - SIGMA)
        for k, value in enumerate(found):
            coef_ref[k, z] = jnp.where(inside, value * (1.0 / THETA), 0.0)
        return carry

    lax.fori_loop(1, WIDE - 1, faces, 0)


def outside(at):
    return max(0, S - at, at - (S + SIDE - 1))


def power_row(source_ref, target_ref, coef_ref, z, reach):
    lane = lane_index((R, LANES))
    first, last = lane == 0, lane == LANES - 1
    for x in range(S - reach, S + SIDE + reach):
        center = [source_ref[z, x, t] for t in range(2)]
        for t in range(1 if outside(x) == reach else 2):
            row = t * HALF + x
            here, there = center[t], center[1 - t]
            before = pltpu.roll(jnp.where(last, there, here), 1, 1)
            after = pltpu.roll(jnp.where(first, there, here), LANES - 1, 1)

            def weight(k):
                return jnp.broadcast_to(coef_ref[k, z, row : row + 1, :], (R, LANES))

            beside = weight(0) * source_ref[z + 1, x, t] + weight(1) * source_ref[z - 1, x, t]
            beside = beside + weight(2) * source_ref[z, x + 1, t]
            beside = beside + weight(3) * source_ref[z, x - 1, t]
            beside = beside + weight(4) * after + weight(5) * before
            target_ref[z, x, t] = weight(6) * here - beside


def power_kernel(
    table_ref,
    own_ref,
    low_ref,
    high_ref,
    mid_ref,
    below_ref,
    above_ref,
    basis_ref,
    moment_ref,
    label_ref,
    cond_ref,
    coef_ref,
    even_ref,
    odd_ref,
):
    blocks = (low_ref, own_ref, high_ref)
    label_ref[...] = jnp.zeros(label_ref.shape, jnp.float32)
    sides = ((0, below_ref), (S, mid_ref), (S + SIDE, above_ref))
    for base, ref in sides:
        for g in range(3):
            for row in range(SIDE):
                labels = (
                    ref[KEPT + 3, g * CELLS + row * SIDE : g * CELLS + (row + 1) * SIDE, :]
                    if g < 2
                    else ref[KEPT + 4, row * SIDE : (row + 1) * SIDE, :]
                )
                label_ref[base + row, g * SIDE : (g + 1) * SIDE, :] = labels
                edge = ref[KEPT + 4, CELLS + g : CELLS + g + 1, :]
                for x in range(SIDE):
                    if outside(base + row) + outside(g * SIDE + x) >= S:
                        continue
                    turn = -((row * SIDE + x) * 2 * S + S) % LANES
                    at = HALF + g * SIDE + x
                    label_ref[base + row, at : at + 1, :] = pltpu.roll(edge, turn, 1)
    coefficients(table_ref, label_ref, cond_ref, coef_ref)

    for row in range(SIDE):
        for x in range(-S, SIDE + S):
            even_ref[S + row, S + x, 0] = blocks[(x + SIDE) // SIDE][row * SIDE + x % SIDE]
    for slot, (row, x) in enumerate(kept_cells((3, 2, 1, 0))):
        even_ref[row, S + x, 0] = below_ref[slot]
    for slot, (row, x) in enumerate(kept_cells((0, 1, 2, 3))):
        even_ref[S + SIDE + row, S + x, 0] = above_ref[slot]
    for base, ref in sides:
        for g in range(3):
            edge = ref[KEPT + g]
            for row in range(SIDE):
                for x in range(SIDE):
                    if outside(base + row) + outside(g * SIDE + x) >= S:
                        continue
                    turn = -((row * SIDE + x) * 2 * S + S) % LANES
                    even_ref[base + row, g * SIDE + x, 1] = pltpu.roll(edge, turn, 1)

    refs = (even_ref, odd_ref)
    for k in range(S + 1):
        now = refs[k % 2]
        for row in range(SIDE):
            for x in range(SIDE):
                basis_ref[k, row * SIDE + x] = now[S + row, S + x, 0]
        if k < S:
            later = refs[1 - k % 2]

            for far in range(S - k):
                reach = S - 1 - k - far

                def one(i, carry):
                    z = S + i if far == 0 else S - far + i * (SIDE - 1 + 2 * far)
                    power_row(now, later, coef_ref, z, reach)
                    return carry

                lax.fori_loop(0, SIDE if far == 0 else 2, one, 0)
    for k in range(S):
        this = jnp.concatenate([basis_ref[k, cell] for cell in range(CELLS)], 1)
        after = jnp.concatenate([basis_ref[k + 1, cell] for cell in range(CELLS)], 1)
        pair = lax.dot_general(
            this,
            jnp.concatenate([this, after], 0),
            (((1,), (1,)), ((), ())),
            precision=lax.Precision.HIGHEST,
            preferred_element_type=jnp.float32,
        )
        half, at = divmod(2 * k * R, LANES)
        moment_ref[half * R : (half + 1) * R, at : at + 2 * R] = pair


def eliminate(mat, right):
    for g in range(S):
        rows = slice(g * R, (g + 1) * R)
        solved, sides = eliminate_rows(mat[rows], right[rows], g * R)
        both = jnp.concatenate([solved, sides], 1)
        taken = jnp.dot(
            mat[:, rows],
            both,
            precision=lax.Precision.HIGHEST,
            preferred_element_type=jnp.float32,
        )
        parts = []
        for h in range(S):
            at = slice(h * R, (h + 1) * R)
            parts.append(
                (solved, sides)
                if h == g
                else (mat[at] - taken[at, :LANES], right[at] - taken[at, LANES:])
            )
        mat = jnp.concatenate([part[0] for part in parts], 0)
        right = jnp.concatenate([part[1] for part in parts], 0)
    return right


def eliminate_rows(mat, right, begin):
    count = R // 8
    tiles = [mat[8 * i : 8 * i + 8] for i in range(count)]
    sides = [right[8 * i : 8 * i + 8] for i in range(count)]
    sub = lax.broadcasted_iota(jnp.int32, (8, LANES), 0)

    def spread(row):
        return jnp.broadcast_to(row, (8, LANES))

    for step in range(0, R, 4):
        k = begin + step
        p, s = divmod(step, 8)
        a = [spread(tiles[p][s + i : s + i + 1, :]) for i in range(4)]
        b = [spread(sides[p][s + i : s + i + 1, :]) for i in range(4)]
        e = {(i, j): spread(a[i][:, k + j : k + j + 1]) for i in range(4) for j in range(i, 4)}
        inv = 1.0 / (e[0, 0] * e[1, 1] - e[0, 1] * e[0, 1])
        q00, q01, q11 = e[1, 1] * inv, -e[0, 1] * inv, e[0, 0] * inv
        w = [[q00 * e[0, j] + q01 * e[1, j] for j in (2, 3)], [q01 * e[0, j] + q11 * e[1, j] for j in (2, 3)]]
        c00 = e[2, 2] - (e[0, 2] * w[0][0] + e[1, 2] * w[1][0])
        c01 = e[2, 3] - (e[0, 2] * w[0][1] + e[1, 2] * w[1][1])
        c11 = e[3, 3] - (e[0, 3] * w[0][1] + e[1, 3] * w[1][1])
        inv = 1.0 / (c00 * c11 - c01 * c01)
        d00, d01, d11 = c11 * inv, -c01 * inv, c00 * inv

        def solve(r):
            y0 = r[2] - (w[0][0] * r[0] + w[1][0] * r[1])
            y1 = r[3] - (w[0][1] * r[0] + w[1][1] * r[1])
            x2 = d00 * y0 + d01 * y1
            x3 = d01 * y0 + d11 * y1
            x0 = (q00 * r[0] + q01 * r[1]) - (w[0][0] * x2 + w[0][1] * x3)
            x1 = (q01 * r[0] + q11 * r[1]) - (w[1][0] * x2 + w[1][1] * x3)
            return [x0, x1, x2, x3]

        a, b = solve(a), solve(b)
        for i in range(count):
            col = [spread(tiles[i][:, k + j : k + j + 1]) for j in range(4)]
            tile = tiles[i] - ((col[0] * a[0] + col[1] * a[1]) + (col[2] * a[2] + col[3] * a[3]))
            rest = sides[i] - ((col[0] * b[0] + col[1] * b[1]) + (col[2] * b[2] + col[3] * b[3]))
            if i == p:
                for j in range(4):
                    tile = jnp.where(sub == s + j, a[j], tile)
                    rest = jnp.where(sub == s + j, b[j], rest)
            tiles[i], sides[i] = tile, rest
    return jnp.concatenate(tiles, 0), jnp.concatenate(sides, 0)


def solve_kernel(moment_ref, basis_ref, solution_ref, residual_ref):
    low, high = moment_ref[0:R, :], moment_ref[R : 2 * R, :]
    lane = lane_index((R, LANES))

    def window(first, second, shift):
        if shift == 0:
            return first
        keep = lane < LANES - shift
        turn = LANES - shift
        return jnp.where(keep, pltpu.roll(first, turn, 1), pltpu.roll(second, turn, 1))

    first = THETA * window(low, high, R) + SIGMA * low
    second = THETA * window(high, high, R) + SIGMA * high
    mat = jnp.concatenate([window(first, second, i * R) for i in range(S)], 0)
    mat = 0.5 * (mat + mat.T)
    right = jnp.concatenate([window(low, high, i * R) for i in range(S)], 0)
    coef = eliminate(mat, right)
    zero = jnp.zeros((R, LANES), jnp.float32)
    here = jnp.concatenate([coef, zero], 0)
    there = jnp.concatenate([zero, coef], 0)
    combo = SIGMA * here + THETA * there
    wide = lane_index(here.shape)
    weights = jnp.where(
        wide < R, here, jnp.where(wide < 2 * R, pltpu.roll(combo, R, 1), 0.0)
    )
    weights = jnp.concatenate([weights, jnp.zeros((96, LANES), jnp.float32)], 0)
    weights = weights.T[: 2 * R, : (S + 1) * R]
    for cell in range(CELLS):
        block = jnp.concatenate([basis_ref[k, cell] for k in range(S + 1)], 0)
        taken = lax.dot_general(
            weights,
            block,
            (((1,), (0,)), ((), ())),
            precision=lax.Precision.HIGHEST,
            preferred_element_type=jnp.float32,
        )
        solution_ref[pl.ds(cell, R, stride=CELLS), :] = taken[:R]
        residual_ref[pl.ds(cell, R, stride=CELLS), :] = basis_ref[0, cell] - taken[R:]


def neighbour(value, axis, offset):
    count = lax.axis_size(axis)
    pairs = [(at, at + offset) for at in range(count) if 0 <= at + offset < count]
    return lax.ppermute(value, axis, pairs)


def total(values):
    near = ("gy", "gz")
    parts = lax.axis_size("gy") * lax.axis_size("gz")
    others = lax.axis_size("gx")
    piece = lax.all_to_all(values.reshape(parts, -1, LANES), near, 0, 0).sum(0)
    pieces = lax.all_to_all(jnp.broadcast_to(piece, (others,) + piece.shape), "gx", 0, 0)
    piece = pieces.sum(0)
    pieces = lax.all_to_all(jnp.broadcast_to(piece, (parts,) + piece.shape), near, 0, 0)
    return pieces.reshape(values.shape)


def body(sources, labels, region_table, sweep_index, sweep_gain):
    rows = call(gain_kernel, "gains", [(R, NREG)], [SMEM, VMEM])(sweep_index, sweep_gain.T)[0]
    block, edge = call(
        rhs_kernel, "rhs", [(CELLS + 1, R, LANES), (EDGE_ROWS, LANES)], [VMEM] * 3
    )(rows, sources.reshape(R * CELLS, LANES), labels.reshape(CELLS, LANES))
    before, after = neighbour(edge, "gy", 1), neighbour(edge, "gy", -1)
    block = call(join_kernel, "join", [(CELLS + 2, R, LANES)], [VMEM] * 3)(block, before, after)[0]
    low, high = neighbour(block, "gx", 1), neighbour(block, "gx", -1)
    down, up = call(merge_kernel, "merge", [(PLANES, R, LANES)] * 2, [VMEM] * 3)(
        block, low, high
    )
    below, above = neighbour(up, "gz", 1), neighbour(down, "gz", -1)
    basis, moments = call(
        power_kernel,
        "powers",
        [(S + 1, CELLS, R, LANES), (2 * R, LANES)],
        [SMEM] + [VMEM] * 6,
        [
            pltpu.VMEM((WIDE, 2 * HALF, LANES), jnp.float32),
            pltpu.VMEM((4, WIDE, 2 * HALF, LANES), jnp.float32),
            pltpu.VMEM((7, WIDE, 2 * HALF, LANES), jnp.float32),
            pltpu.VMEM((WIDE, WIDE, 2, R, LANES), jnp.float32),
            pltpu.VMEM((WIDE, WIDE, 2, R, LANES), jnp.float32),
        ],
            24,
    )(region_table.T, block, low, high, down, below, above)
    solution, residual = call(
        solve_kernel, "solve", [(R * CELLS, LANES)] * 2, [VMEM] * 2
    )(total(moments), basis)
    return (solution.reshape(sources.shape), residual.reshape(sources.shape))


def solution(mesh):
    placed = (P(None, "gz", "gx", "gy"), P("gz", "gx", "gy"), P(), P(), P())
    return jax.shard_map(
        body,
        mesh=mesh,
        in_specs=placed,
        out_specs=(P(None, "gz", "gx", "gy"), P(None, "gz", "gx", "gy")),
        check_vma=False,
    )
```

```python
import jax
import jax.numpy as jnp
from jax import lax
from jax.experimental import pallas as pl
from jax.experimental.pallas import tpu as pltpu
from jax.sharding import PartitionSpec as P

S = 4
NREG = 8
R = 32
SIDE = 4
CELLS = SIDE * SIDE
LANES = 128
WIDE = SIDE + 2 * S
HALF = 16
EDGE_ROWS = R + 8
KEPT = sum(SIDE + 2 * (S - d) for d in range(1, S + 1))
PLANES = KEPT + 5


SIGMA = 8.0
THETA = 8.0

VMEM = pl.BlockSpec(memory_space=pltpu.VMEM)
SMEM = pl.BlockSpec(memory_space=pltpu.SMEM)
HBM = pl.BlockSpec(memory_space=pltpu.HBM)


def call(kernel, name, outs, specs, scratch=(), mebi=8):
    return pl.pallas_call(
        kernel,
        name=name,
        out_shape=[jax.ShapeDtypeStruct(shape, jnp.float32) for shape in outs],
        in_specs=specs,
        out_specs=[VMEM] * len(outs),
        scratch_shapes=list(scratch),
        compiler_params=pltpu.CompilerParams(vmem_limit_bytes=mebi * 1024 * 1024),
    )


def lane_index(shape):
    return lax.broadcasted_iota(jnp.int32, shape, len(shape) - 1)


def rhs_kernel(
    index_ref, gain_hbm, source_hbm, label_hbm, block_ref, edge_ref, gain_ref, source_ref, label_ref, sems
):
    copies = [
        pltpu.make_async_copy(gain_hbm, gain_ref, sems.at[0]),
        pltpu.make_async_copy(label_hbm, label_ref, sems.at[1]),
        pltpu.make_async_copy(source_hbm, source_ref, sems.at[2]),
    ]
    for copy in copies:
        copy.start()
    sub = lax.broadcasted_iota(jnp.int32, (R, gain_ref.shape[1]), 0)
    point = jnp.zeros(sub.shape, jnp.int32)
    for j in range(R):
        point = jnp.where(sub == j, index_ref[j], point)
    copies[0].wait()
    rows = lax.dot_general(
        (point == lane_index(point.shape)).astype(jnp.float32),
        gain_ref[...],
        (((1,), (1,)), ((), ())),
        precision=lax.Precision.HIGHEST,
        preferred_element_type=jnp.float32,
    )
    copies[1].wait()
    copies[2].wait()
    columns = [jnp.broadcast_to(rows[:, k : k + 1], (R, LANES)) for k in range(NREG)]
    group = lane_index((R, LANES)) // (2 * S)
    group_row = lane_index((8, LANES)) // (2 * S)
    edge = jnp.zeros((R, LANES), jnp.float32)
    edge_label = jnp.zeros((8, LANES), jnp.float32)
    labels = label_ref[...].astype(jnp.float32)
    for cell in range(CELLS):
        label = jnp.broadcast_to(labels[cell : cell + 1, :], (R, LANES))
        gain = jnp.zeros((R, LANES), jnp.float32)
        for k in range(NREG):
            gain = jnp.where(label == k + 1.0, columns[k], gain)
        rhs = source_ref[pl.ds(cell, R, stride=CELLS), :] * gain
        block_ref[cell] = rhs
        turn = (cell * 2 * S + S) % LANES
        edge = jnp.where(group == cell, pltpu.roll(rhs, turn, 1), edge)
        edge_label = jnp.where(
            group_row == cell, pltpu.roll(label[:8], turn, 1), edge_label
        )
    block_ref[CELLS, 0:CELLS, :] = labels
    block_ref[CELLS, CELLS:R, :] = jnp.zeros((R - CELLS, LANES), jnp.float32)
    edge_ref[0:R, :] = edge
    edge_ref[R:EDGE_ROWS, :] = edge_label


def join_kernel(block_ref, before_ref, after_ref, out_ref):
    left = lane_index((EDGE_ROWS, LANES)) % (2 * S) < S
    edge = jnp.where(left, before_ref[...], after_ref[...])
    out_ref[0 : CELLS + 1] = block_ref[...]
    out_ref[CELLS, CELLS : CELLS + 1, :] = edge[R : R + 1]
    out_ref[CELLS + 1] = edge[:R]


def kept_cells(order):
    return [
        (row, x)
        for d, row in zip(range(1, S + 1), order)
        for x in range(-(S - d), SIDE + S - d)
    ]


def merge_kernel(own_ref, low_ref, high_ref, down_ref, up_ref):
    blocks = (low_ref, own_ref, high_ref)
    for out_ref, order in ((down_ref, (0, 1, 2, 3)), (up_ref, (3, 2, 1, 0))):
        for slot, (row, x) in enumerate(kept_cells(order)):
            out_ref[slot] = blocks[(x + SIDE) // SIDE][row * SIDE + x % SIDE]
        for g in range(3):
            out_ref[KEPT + g] = blocks[g][CELLS + 1]
            labels = blocks[g][CELLS, 0:CELLS, :]
            if g < 2:
                out_ref[KEPT + 3, g * CELLS : (g + 1) * CELLS, :] = labels
            else:
                out_ref[KEPT + 4, 0:CELLS, :] = labels
            edge = blocks[g][CELLS, CELLS : CELLS + 1, :]
            out_ref[KEPT + 4, CELLS + g : CELLS + g + 1, :] = edge
        out_ref[KEPT + 4, CELLS + 3 : R, :] = jnp.zeros((R - CELLS - 3, LANES), jnp.float32)


def coefficients(table_ref, label_ref, cond_ref, coef_ref):
    def conduct(z, carry):
        label = label_ref[z]
        fields = [jnp.zeros((2 * HALF, LANES), jnp.float32) for _ in range(4)]
        for region in range(NREG):
            hit = label == region + 1.0
            fields = [
                jnp.where(hit, table_ref[column, region], fields[column]) for column in range(4)
            ]
        for column in range(4):
            cond_ref[column, z] = fields[column]
        return carry

    lax.fori_loop(0, WIDE, conduct, 0)
    lane = lane_index((2 * HALF, LANES))

    def faces(z, carry):
        inside = label_ref[z] > 0.5
        along_z, along_x, along_y, shunt = (cond_ref[column, z] for column in range(4))
        after = pltpu.roll(along_y, LANES - 1, 1)
        before = pltpu.roll(along_y, 1, 1)
        after = jnp.where(lane == LANES - 1, pltpu.roll(after, HALF, 0), after)
        before = jnp.where(lane == 0, pltpu.roll(before, HALF, 0), before)
        found = [
            0.5 * (along_z + cond_ref[0, z + 1]),
            0.5 * (along_z + cond_ref[0, z - 1]),
            0.5 * (along_x + pltpu.roll(along_x, 2 * HALF - 1, 0)),
            0.5 * (along_x + pltpu.roll(along_x, 1, 0)),
            0.5 * (along_y + after),
            0.5 * (along_y + before),
        ]
        diag = shunt
        for face in found:
            diag = diag + face
        found.append(diag - SIGMA)
        for k, value in enumerate(found):
            coef_ref[k, z] = jnp.where(inside, value * (1.0 / THETA), 0.0)
        return carry

    lax.fori_loop(1, WIDE - 1, faces, 0)


def outside(at):
    return max(0, S - at, at - (S + SIDE - 1))


def power_row(source_ref, target_ref, coef_ref, z, reach):
    lane = lane_index((R, LANES))
    first, last = lane == 0, lane == LANES - 1
    for x in range(S - reach, S + SIDE + reach):
        center = [source_ref[z, x, t] for t in range(2)]
        for t in range(1 if outside(x) == reach else 2):
            row = t * HALF + x
            here, there = center[t], center[1 - t]
            before = pltpu.roll(jnp.where(last, there, here), 1, 1)
            after = pltpu.roll(jnp.where(first, there, here), LANES - 1, 1)

            def weight(k):
                return jnp.broadcast_to(coef_ref[k, z, row : row + 1, :], (R, LANES))

            beside = weight(0) * source_ref[z + 1, x, t] + weight(1) * source_ref[z - 1, x, t]
            beside = beside + weight(2) * source_ref[z, x + 1, t]
            beside = beside + weight(3) * source_ref[z, x - 1, t]
            beside = beside + weight(4) * after + weight(5) * before
            target_ref[z, x, t] = weight(6) * here - beside


def power_kernel(
    table_ref,
    own_ref,
    low_ref,
    high_ref,
    mid_ref,
    below_ref,
    above_ref,
    basis_ref,
    moment_ref,
    label_ref,
    cond_ref,
    coef_ref,
    even_ref,
    odd_ref,
):
    blocks = (low_ref, own_ref, high_ref)
    label_ref[...] = jnp.zeros(label_ref.shape, jnp.float32)
    sides = ((0, below_ref), (S, mid_ref), (S + SIDE, above_ref))
    for base, ref in sides:
        for g in range(3):
            for row in range(SIDE):
                labels = (
                    ref[KEPT + 3, g * CELLS + row * SIDE : g * CELLS + (row + 1) * SIDE, :]
                    if g < 2
                    else ref[KEPT + 4, row * SIDE : (row + 1) * SIDE, :]
                )
                label_ref[base + row, g * SIDE : (g + 1) * SIDE, :] = labels
                edge = ref[KEPT + 4, CELLS + g : CELLS + g + 1, :]
                for x in range(SIDE):
                    if outside(base + row) + outside(g * SIDE + x) >= S:
                        continue
                    turn = -((row * SIDE + x) * 2 * S + S) % LANES
                    at = HALF + g * SIDE + x
                    label_ref[base + row, at : at + 1, :] = pltpu.roll(edge, turn, 1)
    coefficients(table_ref, label_ref, cond_ref, coef_ref)

    for row in range(SIDE):
        for x in range(-S, SIDE + S):
            even_ref[S + row, S + x, 0] = blocks[(x + SIDE) // SIDE][row * SIDE + x % SIDE]
    for slot, (row, x) in enumerate(kept_cells((3, 2, 1, 0))):
        even_ref[row, S + x, 0] = below_ref[slot]
    for slot, (row, x) in enumerate(kept_cells((0, 1, 2, 3))):
        even_ref[S + SIDE + row, S + x, 0] = above_ref[slot]
    for base, ref in sides:
        for g in range(3):
            edge = ref[KEPT + g]
            for row in range(SIDE):
                for x in range(SIDE):
                    if outside(base + row) + outside(g * SIDE + x) >= S:
                        continue
                    turn = -((row * SIDE + x) * 2 * S + S) % LANES
                    even_ref[base + row, g * SIDE + x, 1] = pltpu.roll(edge, turn, 1)

    def keep(k):
        for row in range(SIDE):
            for x in range(SIDE):
                basis_ref[k, row * SIDE + x] = refs[k % 2][S + row, S + x, 0]

    def moments(k):
        this = jnp.concatenate([basis_ref[k, cell] for cell in range(CELLS)], 1)
        after = jnp.concatenate([basis_ref[k + 1, cell] for cell in range(CELLS)], 1)
        pair = lax.dot_general(
            this,
            jnp.concatenate([this, after], 0),
            (((1,), (1,)), ((), ())),
            precision=lax.Precision.HIGHEST,
            preferred_element_type=jnp.float32,
        )
        half, at = divmod(2 * k * R, LANES)
        moment_ref[half * R : (half + 1) * R, at : at + 2 * R] = pair

    refs = (even_ref, odd_ref)
    keep(0)
    for k in range(S - 1):
        now, later = refs[k % 2], refs[1 - k % 2]
        for far in range(S - k):
            reach = S - 1 - k - far

            def one(i, carry):
                z = S + i if far == 0 else S - far + i * (SIDE - 1 + 2 * far)
                power_row(now, later, coef_ref, z, reach)
                return carry

            lax.fori_loop(0, SIDE if far == 0 else 2, one, 0)
        keep(k + 1)
    for k in range(S - 1):
        moments(k)
    for row in range(SIDE):
        power_row(refs[(S - 1) % 2], refs[S % 2], coef_ref, S + row, 0)
    keep(S)
    moments(S - 1)


def eliminate(mat, right):
    for g in range(S):
        rows = slice(g * R, (g + 1) * R)
        solved, sides = eliminate_rows(mat[rows], right[rows], g * R)
        both = jnp.concatenate([solved, sides], 1)
        taken = jnp.dot(
            mat[:, rows],
            both,
            precision=lax.Precision.HIGHEST,
            preferred_element_type=jnp.float32,
        )
        parts = []
        for h in range(S):
            at = slice(h * R, (h + 1) * R)
            parts.append(
                (solved, sides)
                if h == g
                else (mat[at] - taken[at, :LANES], right[at] - taken[at, LANES:])
            )
        mat = jnp.concatenate([part[0] for part in parts], 0)
        right = jnp.concatenate([part[1] for part in parts], 0)
    return right


def eliminate_rows(mat, right, begin):
    count = R // 8
    tiles = [mat[8 * i : 8 * i + 8] for i in range(count)]
    sides = [right[8 * i : 8 * i + 8] for i in range(count)]
    sub = lax.broadcasted_iota(jnp.int32, (8, LANES), 0)

    def spread(row):
        return jnp.broadcast_to(row, (8, LANES))

    for p in range(count):
        k = begin + 8 * p
        a = [spread(tiles[p][i : i + 1, :]) for i in range(8)]
        b = [spread(sides[p][i : i + 1, :]) for i in range(8)]
        e = {(i, j): spread(a[i][:, k + j : k + j + 1]) for i in range(8) for j in range(i, 8)}
        upper = {}
        for m in range(0, 8, 2):
            n = m + 1
            inv = 1.0 / (e[m, m] * e[n, n] - e[m, n] * e[m, n])
            q00, q01, q11 = e[n, n] * inv, -e[m, n] * inv, e[m, m] * inv
            for j in range(m + 2, 8):
                upper[m, j] = q00 * e[m, j] + q01 * e[n, j]
                upper[n, j] = q01 * e[m, j] + q11 * e[n, j]
            for i in range(m + 2, 8):
                for j in range(i, 8):
                    e[i, j] = e[i, j] - (e[m, i] * upper[m, j] + e[n, i] * upper[n, j])
            for rows in (a, b):
                for j in range(m + 2, 8):
                    rows[j] = rows[j] - (upper[m, j] * rows[m] + upper[n, j] * rows[n])
                rows[m], rows[n] = q00 * rows[m] + q01 * rows[n], q01 * rows[m] + q11 * rows[n]
        for rows in (a, b):
            for m in range(6, 0, -2):
                for i in range(m):
                    rows[i] = rows[i] - (upper[i, m] * rows[m] + upper[i, m + 1] * rows[m + 1])
        for i in range(count):
            if i == p:
                continue
            col = [spread(tiles[i][:, k + j : k + j + 1]) for j in range(8)]
            for parts, rows in ((tiles, a), (sides, b)):
                terms = [col[j] * rows[j] for j in range(8)]
                pairs = [terms[j] + terms[j + 1] for j in range(0, 8, 2)]
                parts[i] = parts[i] - ((pairs[0] + pairs[1]) + (pairs[2] + pairs[3]))
        for parts, rows in ((tiles, a), (sides, b)):
            merged = rows[0]
            for j in range(1, 8):
                merged = jnp.where(sub == j, rows[j], merged)
            parts[p] = merged
    return jnp.concatenate(tiles, 0), jnp.concatenate(sides, 0)


def solve_kernel(moment_ref, basis_ref, solution_ref, residual_ref):
    low, high = moment_ref[0:R, :], moment_ref[R : 2 * R, :]
    lane = lane_index((R, LANES))

    def window(first, second, shift):
        if shift == 0:
            return first
        keep = lane < LANES - shift
        turn = LANES - shift
        return jnp.where(keep, pltpu.roll(first, turn, 1), pltpu.roll(second, turn, 1))

    first = THETA * window(low, high, R) + SIGMA * low
    second = THETA * window(high, high, R) + SIGMA * high
    mat = jnp.concatenate([window(first, second, i * R) for i in range(S)], 0)
    mat = 0.5 * (mat + mat.T)
    right = jnp.concatenate([window(low, high, i * R) for i in range(S)], 0)
    coef = eliminate(mat, right)
    zero = jnp.zeros((R, LANES), jnp.float32)
    here = jnp.concatenate([coef, zero], 0)
    there = jnp.concatenate([zero, coef], 0)
    combo = SIGMA * here + THETA * there
    wide = lane_index(here.shape)
    weights = jnp.where(
        wide < R, here, jnp.where(wide < 2 * R, pltpu.roll(combo, R, 1), 0.0)
    )
    weights = jnp.concatenate([weights, jnp.zeros((96, LANES), jnp.float32)], 0)
    weights = weights.T[: 2 * R, : (S + 1) * R]
    for cell in range(CELLS):
        block = jnp.concatenate([basis_ref[k, cell] for k in range(S + 1)], 0)
        taken = lax.dot_general(
            weights,
            block,
            (((1,), (0,)), ((), ())),
            precision=lax.Precision.HIGHEST,
            preferred_element_type=jnp.float32,
        )
        solution_ref[pl.ds(cell, R, stride=CELLS), :] = taken[:R]
        residual_ref[pl.ds(cell, R, stride=CELLS), :] = basis_ref[0, cell] - taken[R:]


def neighbour(value, axis, offset):
    count = lax.axis_size(axis)
    pairs = [(at, at + offset) for at in range(count) if 0 <= at + offset < count]
    return lax.ppermute(value, axis, pairs)


def total(values):
    near = ("gy", "gz")
    parts = lax.axis_size("gy") * lax.axis_size("gz")
    others = lax.axis_size("gx")
    piece = lax.all_to_all(values.reshape(parts, -1, LANES), near, 0, 0).sum(0)
    pieces = lax.all_to_all(jnp.broadcast_to(piece, (others,) + piece.shape), "gx", 0, 0)
    piece = pieces.sum(0)
    pieces = lax.all_to_all(jnp.broadcast_to(piece, (parts,) + piece.shape), near, 0, 0)
    return pieces.reshape(values.shape)


def body(sources, labels, region_table, sweep_index, sweep_gain):
    block, edge = call(
        rhs_kernel,
        "rhs",
        [(CELLS + 1, R, LANES), (EDGE_ROWS, LANES)],
        [SMEM, HBM, HBM, HBM],
        [
            pltpu.VMEM((NREG, sweep_gain.shape[0]), jnp.float32),
            pltpu.VMEM((R * CELLS, LANES), jnp.float32),
            pltpu.VMEM((CELLS, LANES), jnp.int32),
            pltpu.SemaphoreType.DMA((3,)),
        ],
        60,
    )(sweep_index, sweep_gain.T, sources.reshape(R * CELLS, LANES), labels.reshape(CELLS, LANES))
    before, after = neighbour(edge, "gy", 1), neighbour(edge, "gy", -1)
    block = call(join_kernel, "join", [(CELLS + 2, R, LANES)], [VMEM] * 3)(block, before, after)[0]
    low, high = neighbour(block, "gx", 1), neighbour(block, "gx", -1)
    down, up = call(merge_kernel, "merge", [(PLANES, R, LANES)] * 2, [VMEM] * 3)(
        block, low, high
    )
    below, above = neighbour(up, "gz", 1), neighbour(down, "gz", -1)
    basis, moments = call(
        power_kernel,
        "powers",
        [(S + 1, CELLS, R, LANES), (2 * R, LANES)],
        [SMEM] + [VMEM] * 6,
        [
            pltpu.VMEM((WIDE, 2 * HALF, LANES), jnp.float32),
            pltpu.VMEM((4, WIDE, 2 * HALF, LANES), jnp.float32),
            pltpu.VMEM((7, WIDE, 2 * HALF, LANES), jnp.float32),
            pltpu.VMEM((WIDE, WIDE, 2, R, LANES), jnp.float32),
            pltpu.VMEM((WIDE, WIDE, 2, R, LANES), jnp.float32),
        ],
            24,
    )(region_table.T, block, low, high, down, below, above)
    solution, residual = call(
        solve_kernel, "solve", [(R * CELLS, LANES)] * 2, [VMEM] * 2
    )(total(moments), basis)
    return (solution.reshape(sources.shape), residual.reshape(sources.shape))


def solution(mesh):
    placed = (P(None, "gz", "gx", "gy"), P("gz", "gx", "gy"), P(), P(), P())
    return jax.shard_map(
        body,
        mesh=mesh,
        in_specs=placed,
        out_specs=(P(None, "gz", "gx", "gy"), P(None, "gz", "gx", "gy")),
        check_vma=False,
    )
```

```python
import jax
import jax.numpy as jnp
from jax import lax
from jax.experimental import pallas as pl
from jax.experimental.pallas import tpu as pltpu
from jax.sharding import PartitionSpec as P

S = 4
NREG = 8
R = 32
SIDE = 4
CELLS = SIDE * SIDE
LANES = 128
WIDE = SIDE + 2 * S
HALF = 16
EDGE_ROWS = R + 8
KEPT = sum(SIDE + 2 * (S - d) for d in range(1, S + 1))
PLANES = KEPT + 5


SIGMA = 8.0
THETA = 8.0

VMEM = pl.BlockSpec(memory_space=pltpu.VMEM)
SMEM = pl.BlockSpec(memory_space=pltpu.SMEM)
HBM = pl.BlockSpec(memory_space=pltpu.HBM)


def call(kernel, name, outs, specs, scratch=(), mebi=8):
    return pl.pallas_call(
        kernel,
        name=name,
        out_shape=[jax.ShapeDtypeStruct(shape, jnp.float32) for shape in outs],
        in_specs=specs,
        out_specs=[VMEM] * len(outs),
        scratch_shapes=list(scratch),
        compiler_params=pltpu.CompilerParams(vmem_limit_bytes=mebi * 1024 * 1024),
    )


def lane_index(shape):
    return lax.broadcasted_iota(jnp.int32, shape, len(shape) - 1)


def rhs_kernel(
    index_ref, gain_hbm, source_hbm, label_hbm, block_ref, edge_ref, gain_ref, source_ref, label_ref, sems
):
    copies = [
        pltpu.make_async_copy(gain_hbm, gain_ref, sems.at[0]),
        pltpu.make_async_copy(label_hbm, label_ref, sems.at[1]),
        pltpu.make_async_copy(source_hbm, source_ref, sems.at[2]),
    ]
    for copy in copies:
        copy.start()
    sub = lax.broadcasted_iota(jnp.int32, (R, gain_ref.shape[1]), 0)
    point = jnp.zeros(sub.shape, jnp.int32)
    for j in range(R):
        point = jnp.where(sub == j, index_ref[j], point)
    copies[0].wait()
    rows = lax.dot_general(
        (point == lane_index(point.shape)).astype(jnp.float32),
        gain_ref[...],
        (((1,), (1,)), ((), ())),
        precision=lax.Precision.HIGHEST,
        preferred_element_type=jnp.float32,
    )
    copies[1].wait()
    copies[2].wait()
    columns = [jnp.broadcast_to(rows[:, k : k + 1], (R, LANES)) for k in range(NREG)]
    group = lane_index((R, LANES)) // (2 * S)
    group_row = lane_index((8, LANES)) // (2 * S)
    edge = jnp.zeros((R, LANES), jnp.float32)
    edge_label = jnp.zeros((8, LANES), jnp.float32)
    labels = label_ref[...].astype(jnp.float32)
    for cell in range(CELLS):
        label = jnp.broadcast_to(labels[cell : cell + 1, :], (R, LANES))
        gain = jnp.zeros((R, LANES), jnp.float32)
        for k in range(NREG):
            gain = jnp.where(label == k + 1.0, columns[k], gain)
        rhs = source_ref[pl.ds(cell, R, stride=CELLS), :] * gain
        block_ref[cell] = rhs
        turn = (cell * 2 * S + S) % LANES
        edge = jnp.where(group == cell, pltpu.roll(rhs, turn, 1), edge)
        edge_label = jnp.where(
            group_row == cell, pltpu.roll(label[:8], turn, 1), edge_label
        )
    block_ref[CELLS, 0:CELLS, :] = labels
    block_ref[CELLS, CELLS:R, :] = jnp.zeros((R - CELLS, LANES), jnp.float32)
    for slot in range(edge_ref.shape[0]):
        edge_ref[slot, 0:R, :] = edge
        edge_ref[slot, R:EDGE_ROWS, :] = edge_label


def join_kernel(block_ref, edges_ref, out_ref):
    count = edges_ref.shape[0]
    place = lax.axis_index("gy")
    left = lane_index((EDGE_ROWS, LANES)) % (2 * S) < S
    before = jnp.where(place > 0, edges_ref[jnp.maximum(place - 1, 0)], 0.0)
    after = jnp.where(place < count - 1, edges_ref[jnp.minimum(place + 1, count - 1)], 0.0)
    edge = jnp.where(left, before, after)
    out_ref[0 : CELLS + 1] = block_ref[...]
    out_ref[CELLS, CELLS : CELLS + 1, :] = edge[R : R + 1]
    out_ref[CELLS + 1] = edge[:R]


def kept_cells(order):
    return [
        (row, x)
        for d, row in zip(range(1, S + 1), order)
        for x in range(-(S - d), SIDE + S - d)
    ]


def merge_kernel(own_ref, low_ref, high_ref, down_ref, up_ref):
    blocks = (low_ref, own_ref, high_ref)
    for out_ref, order in ((down_ref, (0, 1, 2, 3)), (up_ref, (3, 2, 1, 0))):
        for slot, (row, x) in enumerate(kept_cells(order)):
            out_ref[slot] = blocks[(x + SIDE) // SIDE][row * SIDE + x % SIDE]
        for g in range(3):
            out_ref[KEPT + g] = blocks[g][CELLS + 1]
            labels = blocks[g][CELLS, 0:CELLS, :]
            if g < 2:
                out_ref[KEPT + 3, g * CELLS : (g + 1) * CELLS, :] = labels
            else:
                out_ref[KEPT + 4, 0:CELLS, :] = labels
            edge = blocks[g][CELLS, CELLS : CELLS + 1, :]
            out_ref[KEPT + 4, CELLS + g : CELLS + g + 1, :] = edge
        out_ref[KEPT + 4, CELLS + 3 : R, :] = jnp.zeros((R - CELLS - 3, LANES), jnp.float32)


def coefficients(table_ref, label_ref, cond_ref, coef_ref):
    def conduct(z, carry):
        label = label_ref[z]
        fields = [jnp.zeros((2 * HALF, LANES), jnp.float32) for _ in range(4)]
        for region in range(NREG):
            hit = label == region + 1.0
            fields = [
                jnp.where(hit, table_ref[column, region], fields[column]) for column in range(4)
            ]
        for column in range(4):
            cond_ref[column, z] = fields[column]
        return carry

    lax.fori_loop(0, WIDE, conduct, 0)
    lane = lane_index((2 * HALF, LANES))

    def faces(z, carry):
        inside = label_ref[z] > 0.5
        along_z, along_x, along_y, shunt = (cond_ref[column, z] for column in range(4))
        after = pltpu.roll(along_y, LANES - 1, 1)
        before = pltpu.roll(along_y, 1, 1)
        after = jnp.where(lane == LANES - 1, pltpu.roll(after, HALF, 0), after)
        before = jnp.where(lane == 0, pltpu.roll(before, HALF, 0), before)
        found = [
            0.5 * (along_z + cond_ref[0, z + 1]),
            0.5 * (along_z + cond_ref[0, z - 1]),
            0.5 * (along_x + pltpu.roll(along_x, 2 * HALF - 1, 0)),
            0.5 * (along_x + pltpu.roll(along_x, 1, 0)),
            0.5 * (along_y + after),
            0.5 * (along_y + before),
        ]
        diag = shunt
        for face in found:
            diag = diag + face
        found.append(diag - SIGMA)
        for k, value in enumerate(found):
            coef_ref[k, z] = jnp.where(inside, value * (1.0 / THETA), 0.0)
        return carry

    lax.fori_loop(1, WIDE - 1, faces, 0)


def outside(at):
    return max(0, S - at, at - (S + SIDE - 1))


def power_row(source_ref, target_ref, coef_ref, z, reach):
    lane = lane_index((R, LANES))
    first, last = lane == 0, lane == LANES - 1
    for x in range(S - reach, S + SIDE + reach):
        center = [source_ref[z, x, t] for t in range(2)]
        for t in range(1 if outside(x) == reach else 2):
            row = t * HALF + x
            here, there = center[t], center[1 - t]
            before = pltpu.roll(jnp.where(last, there, here), 1, 1)
            after = pltpu.roll(jnp.where(first, there, here), LANES - 1, 1)

            def weight(k):
                return jnp.broadcast_to(coef_ref[k, z, row : row + 1, :], (R, LANES))

            beside = weight(0) * source_ref[z + 1, x, t] + weight(1) * source_ref[z - 1, x, t]
            beside = beside + weight(2) * source_ref[z, x + 1, t]
            beside = beside + weight(3) * source_ref[z, x - 1, t]
            beside = beside + weight(4) * after + weight(5) * before
            target_ref[z, x, t] = weight(6) * here - beside


def power_kernel(
    table_ref,
    own_ref,
    low_ref,
    high_ref,
    mid_ref,
    below_ref,
    above_ref,
    basis_ref,
    moment_ref,
    label_ref,
    cond_ref,
    coef_ref,
    even_ref,
    odd_ref,
):
    blocks = (low_ref, own_ref, high_ref)
    label_ref[...] = jnp.zeros(label_ref.shape, jnp.float32)
    sides = ((0, below_ref), (S, mid_ref), (S + SIDE, above_ref))
    for base, ref in sides:
        for g in range(3):
            for row in range(SIDE):
                labels = (
                    ref[KEPT + 3, g * CELLS + row * SIDE : g * CELLS + (row + 1) * SIDE, :]
                    if g < 2
                    else ref[KEPT + 4, row * SIDE : (row + 1) * SIDE, :]
                )
                label_ref[base + row, g * SIDE : (g + 1) * SIDE, :] = labels
                edge = ref[KEPT + 4, CELLS + g : CELLS + g + 1, :]
                for x in range(SIDE):
                    if outside(base + row) + outside(g * SIDE + x) >= S:
                        continue
                    turn = -((row * SIDE + x) * 2 * S + S) % LANES
                    at = HALF + g * SIDE + x
                    label_ref[base + row, at : at + 1, :] = pltpu.roll(edge, turn, 1)
    coefficients(table_ref, label_ref, cond_ref, coef_ref)

    for row in range(SIDE):
        for x in range(-S, SIDE + S):
            even_ref[S + row, S + x, 0] = blocks[(x + SIDE) // SIDE][row * SIDE + x % SIDE]
    for slot, (row, x) in enumerate(kept_cells((3, 2, 1, 0))):
        even_ref[row, S + x, 0] = below_ref[slot]
    for slot, (row, x) in enumerate(kept_cells((0, 1, 2, 3))):
        even_ref[S + SIDE + row, S + x, 0] = above_ref[slot]
    for base, ref in sides:
        for g in range(3):
            edge = ref[KEPT + g]
            for row in range(SIDE):
                for x in range(SIDE):
                    if outside(base + row) + outside(g * SIDE + x) >= S:
                        continue
                    turn = -((row * SIDE + x) * 2 * S + S) % LANES
                    even_ref[base + row, g * SIDE + x, 1] = pltpu.roll(edge, turn, 1)

    def keep(k):
        for row in range(SIDE):
            for x in range(SIDE):
                basis_ref[k, row * SIDE + x] = refs[k % 2][S + row, S + x, 0]

    def moments(k):
        this = jnp.concatenate([basis_ref[k, cell] for cell in range(CELLS)], 1)
        after = jnp.concatenate([basis_ref[k + 1, cell] for cell in range(CELLS)], 1)
        pair = lax.dot_general(
            this,
            jnp.concatenate([this, after], 0),
            (((1,), (1,)), ((), ())),
            precision=lax.Precision.HIGHEST,
            preferred_element_type=jnp.float32,
        )
        half, at = divmod(2 * k * R, LANES)
        moment_ref[half * R : (half + 1) * R, at : at + 2 * R] = pair

    refs = (even_ref, odd_ref)
    keep(0)
    for k in range(S - 1):
        now, later = refs[k % 2], refs[1 - k % 2]
        for far in range(S - k):
            reach = S - 1 - k - far

            def one(i, carry):
                z = S + i if far == 0 else S - far + i * (SIDE - 1 + 2 * far)
                power_row(now, later, coef_ref, z, reach)
                return carry

            lax.fori_loop(0, SIDE if far == 0 else 2, one, 0)
        keep(k + 1)
    for k in range(S - 1):
        moments(k)
    for row in range(SIDE):
        power_row(refs[(S - 1) % 2], refs[S % 2], coef_ref, S + row, 0)
    keep(S)
    moments(S - 1)


def eliminate(mat, right):
    for g in range(S):
        rows = slice(g * R, (g + 1) * R)
        solved, sides = eliminate_rows(mat[rows], right[rows], g * R)
        both = jnp.concatenate([solved, sides], 1)
        taken = jnp.dot(
            mat[:, rows],
            both,
            precision=lax.Precision.HIGHEST,
            preferred_element_type=jnp.float32,
        )
        parts = []
        for h in range(S):
            at = slice(h * R, (h + 1) * R)
            parts.append(
                (solved, sides)
                if h == g
                else (mat[at] - taken[at, :LANES], right[at] - taken[at, LANES:])
            )
        mat = jnp.concatenate([part[0] for part in parts], 0)
        right = jnp.concatenate([part[1] for part in parts], 0)
    return right


def eliminate_rows(mat, right, begin):
    count = R // 8
    tiles = [mat[8 * i : 8 * i + 8] for i in range(count)]
    sides = [right[8 * i : 8 * i + 8] for i in range(count)]
    sub = lax.broadcasted_iota(jnp.int32, (8, LANES), 0)

    def spread(row):
        return jnp.broadcast_to(row, (8, LANES))

    for p in range(count):
        k = begin + 8 * p
        a = [spread(tiles[p][i : i + 1, :]) for i in range(8)]
        b = [spread(sides[p][i : i + 1, :]) for i in range(8)]
        e = {(i, j): spread(a[i][:, k + j : k + j + 1]) for i in range(8) for j in range(i, 8)}
        upper = {}
        for m in range(0, 8, 2):
            n = m + 1
            inv = 1.0 / (e[m, m] * e[n, n] - e[m, n] * e[m, n])
            q00, q01, q11 = e[n, n] * inv, -e[m, n] * inv, e[m, m] * inv
            for j in range(m + 2, 8):
                upper[m, j] = q00 * e[m, j] + q01 * e[n, j]
                upper[n, j] = q01 * e[m, j] + q11 * e[n, j]
            for i in range(m + 2, 8):
                for j in range(i, 8):
                    e[i, j] = e[i, j] - (e[m, i] * upper[m, j] + e[n, i] * upper[n, j])
            for rows in (a, b):
                for j in range(m + 2, 8):
                    rows[j] = rows[j] - (upper[m, j] * rows[m] + upper[n, j] * rows[n])
                rows[m], rows[n] = q00 * rows[m] + q01 * rows[n], q01 * rows[m] + q11 * rows[n]
        for rows in (a, b):
            for m in range(6, 0, -2):
                for i in range(m):
                    rows[i] = rows[i] - (upper[i, m] * rows[m] + upper[i, m + 1] * rows[m + 1])
        for i in range(count):
            if i == p:
                continue
            col = [spread(tiles[i][:, k + j : k + j + 1]) for j in range(8)]
            for parts, rows in ((tiles, a), (sides, b)):
                terms = [col[j] * rows[j] for j in range(8)]
                pairs = [terms[j] + terms[j + 1] for j in range(0, 8, 2)]
                parts[i] = parts[i] - ((pairs[0] + pairs[1]) + (pairs[2] + pairs[3]))
        for parts, rows in ((tiles, a), (sides, b)):
            merged = rows[0]
            for j in range(1, 8):
                merged = jnp.where(sub == j, rows[j], merged)
            parts[p] = merged
    return jnp.concatenate(tiles, 0), jnp.concatenate(sides, 0)


def solve_kernel(moment_ref, basis_ref, solution_ref, residual_ref):
    low, high = moment_ref[0:R, :], moment_ref[R : 2 * R, :]
    lane = lane_index((R, LANES))

    def window(first, second, shift):
        if shift == 0:
            return first
        keep = lane < LANES - shift
        turn = LANES - shift
        return jnp.where(keep, pltpu.roll(first, turn, 1), pltpu.roll(second, turn, 1))

    first = THETA * window(low, high, R) + SIGMA * low
    second = THETA * window(high, high, R) + SIGMA * high
    mat = jnp.concatenate([window(first, second, i * R) for i in range(S)], 0)
    mat = 0.5 * (mat + mat.T)
    right = jnp.concatenate([window(low, high, i * R) for i in range(S)], 0)
    coef = eliminate(mat, right)
    zero = jnp.zeros((R, LANES), jnp.float32)
    here = jnp.concatenate([coef, zero], 0)
    there = jnp.concatenate([zero, coef], 0)
    combo = SIGMA * here + THETA * there
    wide = lane_index(here.shape)
    weights = jnp.where(
        wide < R, here, jnp.where(wide < 2 * R, pltpu.roll(combo, R, 1), 0.0)
    )
    weights = jnp.concatenate([weights, jnp.zeros((96, LANES), jnp.float32)], 0)
    weights = weights.T[: 2 * R, : (S + 1) * R]
    for cell in range(CELLS):
        block = jnp.concatenate([basis_ref[k, cell] for k in range(S + 1)], 0)
        taken = lax.dot_general(
            weights,
            block,
            (((1,), (0,)), ((), ())),
            precision=lax.Precision.HIGHEST,
            preferred_element_type=jnp.float32,
        )
        solution_ref[pl.ds(cell, R, stride=CELLS), :] = taken[:R]
        residual_ref[pl.ds(cell, R, stride=CELLS), :] = basis_ref[0, cell] - taken[R:]


def neighbour(value, axis, offset):
    count = lax.axis_size(axis)
    pairs = [(at, at + offset) for at in range(count) if 0 <= at + offset < count]
    return lax.ppermute(value, axis, pairs)


def total(values):
    near = ("gy", "gz")
    parts = lax.axis_size("gy") * lax.axis_size("gz")
    others = lax.axis_size("gx")
    piece = lax.all_to_all(values.reshape(parts, -1, LANES), near, 0, 0).sum(0)
    pieces = lax.all_to_all(jnp.broadcast_to(piece, (others,) + piece.shape), "gx", 0, 0)
    piece = pieces.sum(0)
    pieces = lax.all_to_all(jnp.broadcast_to(piece, (parts,) + piece.shape), near, 0, 0)
    return pieces.reshape(values.shape)


def body(sources, labels, region_table, sweep_index, sweep_gain):
    block, edge = call(
        rhs_kernel,
        "rhs",
        [(CELLS + 1, R, LANES), (lax.axis_size("gy"), EDGE_ROWS, LANES)],
        [SMEM, HBM, HBM, HBM],
        [
            pltpu.VMEM((NREG, sweep_gain.shape[0]), jnp.float32),
            pltpu.VMEM((R * CELLS, LANES), jnp.float32),
            pltpu.VMEM((CELLS, LANES), jnp.int32),
            pltpu.SemaphoreType.DMA((3,)),
        ],
        60,
    )(sweep_index, sweep_gain.T, sources.reshape(R * CELLS, LANES), labels.reshape(CELLS, LANES))
    edges = lax.all_to_all(edge, "gy", 0, 0)
    block = call(join_kernel, "join", [(CELLS + 2, R, LANES)], [VMEM] * 2)(block, edges)[0]
    low, high = neighbour(block, "gx", 1), neighbour(block, "gx", -1)
    down, up = call(merge_kernel, "merge", [(PLANES, R, LANES)] * 2, [VMEM] * 3)(
        block, low, high
    )
    below, above = neighbour(up, "gz", 1), neighbour(down, "gz", -1)
    basis, moments = call(
        power_kernel,
        "powers",
        [(S + 1, CELLS, R, LANES), (2 * R, LANES)],
        [SMEM] + [VMEM] * 6,
        [
            pltpu.VMEM((WIDE, 2 * HALF, LANES), jnp.float32),
            pltpu.VMEM((4, WIDE, 2 * HALF, LANES), jnp.float32),
            pltpu.VMEM((7, WIDE, 2 * HALF, LANES), jnp.float32),
            pltpu.VMEM((WIDE, WIDE, 2, R, LANES), jnp.float32),
            pltpu.VMEM((WIDE, WIDE, 2, R, LANES), jnp.float32),
        ],
            24,
    )(region_table.T, block, low, high, down, below, above)
    solution, residual = call(
        solve_kernel, "solve", [(R * CELLS, LANES)] * 2, [VMEM] * 2
    )(total(moments), basis)
    return (solution.reshape(sources.shape), residual.reshape(sources.shape))


def solution(mesh):
    placed = (P(None, "gz", "gx", "gy"), P("gz", "gx", "gy"), P(), P(), P())
    return jax.shard_map(
        body,
        mesh=mesh,
        in_specs=placed,
        out_specs=(P(None, "gz", "gx", "gy"), P(None, "gz", "gx", "gy")),
        check_vma=False,
    )
```

```python
import jax
import jax.numpy as jnp
from jax import lax
from jax.experimental import pallas as pl
from jax.experimental.pallas import tpu as pltpu
from jax.sharding import PartitionSpec as P

S = 4
NREG = 8
R = 32
SIDE = 4
CELLS = SIDE * SIDE
LANES = 128
WIDE = SIDE + 2 * S
HALF = 16
EDGE_ROWS = R + 8
KEPT = sum(SIDE + 2 * (S - d) for d in range(1, S + 1))
PLANES = KEPT + 5


SIGMA = 8.0
THETA = 8.0

VMEM = pl.BlockSpec(memory_space=pltpu.VMEM)
SMEM = pl.BlockSpec(memory_space=pltpu.SMEM)
HBM = pl.BlockSpec(memory_space=pltpu.HBM)


def call(kernel, name, outs, specs, scratch=(), mebi=8):
    return pl.pallas_call(
        kernel,
        name=name,
        out_shape=[jax.ShapeDtypeStruct(shape, jnp.float32) for shape in outs],
        in_specs=specs,
        out_specs=[VMEM] * len(outs),
        scratch_shapes=list(scratch),
        compiler_params=pltpu.CompilerParams(vmem_limit_bytes=mebi * 1024 * 1024),
    )


def lane_index(shape):
    return lax.broadcasted_iota(jnp.int32, shape, len(shape) - 1)


def rhs_kernel(
    index_ref, gain_hbm, source_hbm, label_hbm, block_ref, edge_ref, gain_ref, source_ref, label_ref, sems
):
    copies = [
        pltpu.make_async_copy(gain_hbm, gain_ref, sems.at[0]),
        pltpu.make_async_copy(label_hbm, label_ref, sems.at[1]),
        pltpu.make_async_copy(source_hbm, source_ref, sems.at[2]),
    ]
    for copy in copies:
        copy.start()
    sub = lax.broadcasted_iota(jnp.int32, (R, gain_ref.shape[1]), 0)
    point = jnp.zeros(sub.shape, jnp.int32)
    for j in range(R):
        point = jnp.where(sub == j, index_ref[j], point)
    copies[0].wait()
    rows = lax.dot_general(
        (point == lane_index(point.shape)).astype(jnp.float32),
        gain_ref[...],
        (((1,), (1,)), ((), ())),
        precision=lax.Precision.HIGHEST,
        preferred_element_type=jnp.float32,
    )
    copies[1].wait()
    copies[2].wait()
    columns = [jnp.broadcast_to(rows[:, k : k + 1], (R, LANES)) for k in range(NREG)]
    group = lane_index((R, LANES)) // (2 * S)
    group_row = lane_index((8, LANES)) // (2 * S)
    edge = jnp.zeros((R, LANES), jnp.float32)
    edge_label = jnp.zeros((8, LANES), jnp.float32)
    labels = label_ref[...].astype(jnp.float32)
    for cell in range(CELLS):
        label = jnp.broadcast_to(labels[cell : cell + 1, :], (R, LANES))
        gain = jnp.zeros((R, LANES), jnp.float32)
        for k in range(NREG):
            gain = jnp.where(label == k + 1.0, columns[k], gain)
        rhs = source_ref[pl.ds(cell, R, stride=CELLS), :] * gain
        block_ref[cell] = rhs
        turn = (cell * 2 * S + S) % LANES
        edge = jnp.where(group == cell, pltpu.roll(rhs, turn, 1), edge)
        edge_label = jnp.where(
            group_row == cell, pltpu.roll(label[:8], turn, 1), edge_label
        )
    block_ref[CELLS, 0:CELLS, :] = labels
    block_ref[CELLS, CELLS:R, :] = jnp.zeros((R - CELLS, LANES), jnp.float32)
    for slot in range(edge_ref.shape[0]):
        edge_ref[slot, 0:R, :] = edge
        edge_ref[slot, R:EDGE_ROWS, :] = edge_label


def join_kernel(block_ref, edges_ref, out_ref):
    count = edges_ref.shape[0]
    place = lax.axis_index("gy")
    left = lane_index((EDGE_ROWS, LANES)) % (2 * S) < S
    before = jnp.where(place > 0, edges_ref[jnp.maximum(place - 1, 0)], 0.0)
    after = jnp.where(place < count - 1, edges_ref[jnp.minimum(place + 1, count - 1)], 0.0)
    edge = jnp.where(left, before, after)
    out_ref[0 : CELLS + 1] = block_ref[...]
    out_ref[CELLS, CELLS : CELLS + 1, :] = edge[R : R + 1]
    out_ref[CELLS + 1] = edge[:R]


def kept_cells(order):
    return [
        (row, x)
        for d, row in zip(range(1, S + 1), order)
        for x in range(-(S - d), SIDE + S - d)
    ]


def merge_kernel(own_ref, low_ref, high_ref, down_ref, up_ref):
    blocks = (low_ref, own_ref, high_ref)
    for out_ref, order in ((down_ref, (0, 1, 2, 3)), (up_ref, (3, 2, 1, 0))):
        for slot, (row, x) in enumerate(kept_cells(order)):
            out_ref[slot] = blocks[(x + SIDE) // SIDE][row * SIDE + x % SIDE]
        for g in range(3):
            out_ref[KEPT + g] = blocks[g][CELLS + 1]
            labels = blocks[g][CELLS, 0:CELLS, :]
            if g < 2:
                out_ref[KEPT + 3, g * CELLS : (g + 1) * CELLS, :] = labels
            else:
                out_ref[KEPT + 4, 0:CELLS, :] = labels
            edge = blocks[g][CELLS, CELLS : CELLS + 1, :]
            out_ref[KEPT + 4, CELLS + g : CELLS + g + 1, :] = edge
        out_ref[KEPT + 4, CELLS + 3 : R, :] = jnp.zeros((R - CELLS - 3, LANES), jnp.float32)


def coefficients(table_ref, label_ref, cond_ref, coef_ref):
    def conduct(z, carry):
        label = label_ref[z]
        fields = [jnp.zeros((2 * HALF, LANES), jnp.float32) for _ in range(4)]
        for region in range(NREG):
            hit = label == region + 1.0
            fields = [
                jnp.where(hit, table_ref[column, region], fields[column]) for column in range(4)
            ]
        for column in range(4):
            cond_ref[column, z] = fields[column]
        return carry

    lax.fori_loop(0, WIDE, conduct, 0, unroll=3)
    lane = lane_index((2 * HALF, LANES))

    def faces(z, carry):
        inside = label_ref[z] > 0.5
        along_z, along_x, along_y, shunt = (cond_ref[column, z] for column in range(4))
        after = pltpu.roll(along_y, LANES - 1, 1)
        before = pltpu.roll(along_y, 1, 1)
        after = jnp.where(lane == LANES - 1, pltpu.roll(after, HALF, 0), after)
        before = jnp.where(lane == 0, pltpu.roll(before, HALF, 0), before)
        found = [
            0.5 * (along_z + cond_ref[0, z + 1]),
            0.5 * (along_z + cond_ref[0, z - 1]),
            0.5 * (along_x + pltpu.roll(along_x, 2 * HALF - 1, 0)),
            0.5 * (along_x + pltpu.roll(along_x, 1, 0)),
            0.5 * (along_y + after),
            0.5 * (along_y + before),
        ]
        diag = shunt
        for face in found:
            diag = diag + face
        found.append(diag - SIGMA)
        for k, value in enumerate(found):
            coef_ref[k, z] = jnp.where(inside, value * (1.0 / THETA), 0.0)
        return carry

    lax.fori_loop(1, WIDE - 1, faces, 0, unroll=5)


def outside(at):
    return max(0, S - at, at - (S + SIDE - 1))


def power_row(source_ref, target_ref, coef_ref, z, reach):
    lane = lane_index((R, LANES))
    first, last = lane == 0, lane == LANES - 1
    for x in range(S - reach, S + SIDE + reach):
        center = [source_ref[z, x, t] for t in range(2)]
        for t in range(1 if outside(x) == reach else 2):
            row = t * HALF + x
            here, there = center[t], center[1 - t]
            before = pltpu.roll(jnp.where(last, there, here), 1, 1)
            after = pltpu.roll(jnp.where(first, there, here), LANES - 1, 1)

            def weight(k):
                return jnp.broadcast_to(coef_ref[k, z, row : row + 1, :], (R, LANES))

            beside = weight(0) * source_ref[z + 1, x, t] + weight(1) * source_ref[z - 1, x, t]
            beside = beside + weight(2) * source_ref[z, x + 1, t]
            beside = beside + weight(3) * source_ref[z, x - 1, t]
            beside = beside + weight(4) * after + weight(5) * before
            target_ref[z, x, t] = weight(6) * here - beside


def power_kernel(
    table_ref,
    own_ref,
    low_ref,
    high_ref,
    mid_ref,
    below_ref,
    above_ref,
    basis_ref,
    moment_ref,
    label_ref,
    cond_ref,
    coef_ref,
    even_ref,
    odd_ref,
):
    blocks = (low_ref, own_ref, high_ref)
    label_ref[...] = jnp.zeros(label_ref.shape, jnp.float32)
    sides = ((0, below_ref), (S, mid_ref), (S + SIDE, above_ref))
    for base, ref in sides:
        for g in range(3):
            for row in range(SIDE):
                labels = (
                    ref[KEPT + 3, g * CELLS + row * SIDE : g * CELLS + (row + 1) * SIDE, :]
                    if g < 2
                    else ref[KEPT + 4, row * SIDE : (row + 1) * SIDE, :]
                )
                label_ref[base + row, g * SIDE : (g + 1) * SIDE, :] = labels
                edge = ref[KEPT + 4, CELLS + g : CELLS + g + 1, :]
                for x in range(SIDE):
                    if outside(base + row) + outside(g * SIDE + x) >= S:
                        continue
                    turn = -((row * SIDE + x) * 2 * S + S) % LANES
                    at = HALF + g * SIDE + x
                    label_ref[base + row, at : at + 1, :] = pltpu.roll(edge, turn, 1)
    coefficients(table_ref, label_ref, cond_ref, coef_ref)

    for row in range(SIDE):
        for x in range(-S, SIDE + S):
            even_ref[S + row, S + x, 0] = blocks[(x + SIDE) // SIDE][row * SIDE + x % SIDE]
    for slot, (row, x) in enumerate(kept_cells((3, 2, 1, 0))):
        even_ref[row, S + x, 0] = below_ref[slot]
    for slot, (row, x) in enumerate(kept_cells((0, 1, 2, 3))):
        even_ref[S + SIDE + row, S + x, 0] = above_ref[slot]
    for base, ref in sides:
        for g in range(3):
            edge = ref[KEPT + g]
            for row in range(SIDE):
                for x in range(SIDE):
                    if outside(base + row) + outside(g * SIDE + x) >= S:
                        continue
                    turn = -((row * SIDE + x) * 2 * S + S) % LANES
                    even_ref[base + row, g * SIDE + x, 1] = pltpu.roll(edge, turn, 1)

    def keep(k):
        for row in range(SIDE):
            for x in range(SIDE):
                basis_ref[k, row * SIDE + x] = refs[k % 2][S + row, S + x, 0]

    def moments(k):
        this = jnp.concatenate([basis_ref[k, cell] for cell in range(CELLS)], 1)
        after = jnp.concatenate([basis_ref[k + 1, cell] for cell in range(CELLS)], 1)
        pair = lax.dot_general(
            this,
            jnp.concatenate([this, after], 0),
            (((1,), (1,)), ((), ())),
            precision=lax.Precision.HIGHEST,
            preferred_element_type=jnp.float32,
        )
        half, at = divmod(2 * k * R, LANES)
        moment_ref[half * R : (half + 1) * R, at : at + 2 * R] = pair

    refs = (even_ref, odd_ref)
    keep(0)
    for k in range(S - 1):
        now, later = refs[k % 2], refs[1 - k % 2]
        for far in range(S - k):
            reach = S - 1 - k - far

            def one(i, carry):
                for z in (S + 2 * i, S + 2 * i + 1):
                    power_row(now, later, coef_ref, z, reach)
                return carry

            if far == 0:
                lax.fori_loop(0, SIDE // 2, one, 0)
            else:
                for z in (S - far, S + SIDE - 1 + far):
                    power_row(now, later, coef_ref, z, reach)
        keep(k + 1)
    for k in range(S - 1):
        moments(k)
    for row in range(SIDE):
        power_row(refs[(S - 1) % 2], refs[S % 2], coef_ref, S + row, 0)
    keep(S)
    moments(S - 1)


def eliminate(mat, right):
    for g in range(S):
        rows = slice(g * R, (g + 1) * R)
        solved, sides = eliminate_rows(mat[rows], right[rows], g * R)
        both = jnp.concatenate([solved, sides], 1)
        taken = jnp.dot(
            mat[:, rows],
            both,
            precision=lax.Precision.HIGHEST,
            preferred_element_type=jnp.float32,
        )
        parts = []
        for h in range(S):
            at = slice(h * R, (h + 1) * R)
            parts.append(
                (solved, sides)
                if h == g
                else (mat[at] - taken[at, :LANES], right[at] - taken[at, LANES:])
            )
        mat = jnp.concatenate([part[0] for part in parts], 0)
        right = jnp.concatenate([part[1] for part in parts], 0)
    return right


def eliminate_rows(mat, right, begin):
    count = R // 8
    tiles = [mat[8 * i : 8 * i + 8] for i in range(count)]
    sides = [right[8 * i : 8 * i + 8] for i in range(count)]
    sub = lax.broadcasted_iota(jnp.int32, (8, LANES), 0)

    def spread(row):
        return jnp.broadcast_to(row, (8, LANES))

    for p in range(count):
        k = begin + 8 * p
        a = [spread(tiles[p][i : i + 1, :]) for i in range(8)]
        b = [spread(sides[p][i : i + 1, :]) for i in range(8)]
        e = {(i, j): spread(a[i][:, k + j : k + j + 1]) for i in range(8) for j in range(i, 8)}
        upper = {}
        for m in range(0, 8, 2):
            n = m + 1
            inv = 1.0 / (e[m, m] * e[n, n] - e[m, n] * e[m, n])
            q00, q01, q11 = e[n, n] * inv, -e[m, n] * inv, e[m, m] * inv
            for j in range(m + 2, 8):
                upper[m, j] = q00 * e[m, j] + q01 * e[n, j]
                upper[n, j] = q01 * e[m, j] + q11 * e[n, j]
            for i in range(m + 2, 8):
                for j in range(i, 8):
                    e[i, j] = e[i, j] - (e[m, i] * upper[m, j] + e[n, i] * upper[n, j])
            for rows in (a, b):
                for j in range(m + 2, 8):
                    rows[j] = rows[j] - (upper[m, j] * rows[m] + upper[n, j] * rows[n])
                rows[m], rows[n] = q00 * rows[m] + q01 * rows[n], q01 * rows[m] + q11 * rows[n]
        for rows in (a, b):
            for m in range(6, 0, -2):
                for i in range(m):
                    rows[i] = rows[i] - (upper[i, m] * rows[m] + upper[i, m + 1] * rows[m + 1])
        for i in range(count):
            if i == p:
                continue
            col = [spread(tiles[i][:, k + j : k + j + 1]) for j in range(8)]
            for parts, rows in ((tiles, a), (sides, b)):
                terms = [col[j] * rows[j] for j in range(8)]
                pairs = [terms[j] + terms[j + 1] for j in range(0, 8, 2)]
                parts[i] = parts[i] - ((pairs[0] + pairs[1]) + (pairs[2] + pairs[3]))
        for parts, rows in ((tiles, a), (sides, b)):
            merged = rows[0]
            for j in range(1, 8):
                merged = jnp.where(sub == j, rows[j], merged)
            parts[p] = merged
    return jnp.concatenate(tiles, 0), jnp.concatenate(sides, 0)


def solve_kernel(moment_ref, basis_ref, solution_ref, residual_ref):
    low, high = moment_ref[0:R, :], moment_ref[R : 2 * R, :]
    lane = lane_index((R, LANES))

    def window(first, second, shift):
        if shift == 0:
            return first
        keep = lane < LANES - shift
        turn = LANES - shift
        return jnp.where(keep, pltpu.roll(first, turn, 1), pltpu.roll(second, turn, 1))

    first = THETA * window(low, high, R) + SIGMA * low
    second = THETA * window(high, high, R) + SIGMA * high
    mat = jnp.concatenate([window(first, second, i * R) for i in range(S)], 0)
    mat = 0.5 * (mat + mat.T)
    right = jnp.concatenate([window(low, high, i * R) for i in range(S)], 0)
    coef = eliminate(mat, right)
    zero = jnp.zeros((R, LANES), jnp.float32)
    here = jnp.concatenate([coef, zero], 0)
    there = jnp.concatenate([zero, coef], 0)
    combo = SIGMA * here + THETA * there
    wide = lane_index(here.shape)
    weights = jnp.where(
        wide < R, here, jnp.where(wide < 2 * R, pltpu.roll(combo, R, 1), 0.0)
    )
    weights = jnp.concatenate([weights, jnp.zeros((96, LANES), jnp.float32)], 0)
    weights = weights.T[: 2 * R, : (S + 1) * R]
    for cell in range(CELLS):
        block = jnp.concatenate([basis_ref[k, cell] for k in range(S + 1)], 0)
        taken = lax.dot_general(
            weights,
            block,
            (((1,), (0,)), ((), ())),
            precision=lax.Precision.HIGHEST,
            preferred_element_type=jnp.float32,
        )
        solution_ref[pl.ds(cell, R, stride=CELLS), :] = taken[:R]
        residual_ref[pl.ds(cell, R, stride=CELLS), :] = basis_ref[0, cell] - taken[R:]


def neighbour(value, axis, offset):
    count = lax.axis_size(axis)
    pairs = [(at, at + offset) for at in range(count) if 0 <= at + offset < count]
    return lax.ppermute(value, axis, pairs)


def total(values):
    near = ("gy", "gz")
    parts = lax.axis_size("gy") * lax.axis_size("gz")
    others = lax.axis_size("gx")
    piece = lax.all_to_all(values.reshape(parts, -1, LANES), near, 0, 0).sum(0)
    pieces = lax.all_to_all(jnp.broadcast_to(piece, (others,) + piece.shape), "gx", 0, 0)
    piece = pieces.sum(0)
    pieces = lax.all_to_all(jnp.broadcast_to(piece, (parts,) + piece.shape), near, 0, 0)
    return pieces.reshape(values.shape)


def body(sources, labels, region_table, sweep_index, sweep_gain):
    block, edge = call(
        rhs_kernel,
        "rhs",
        [(CELLS + 1, R, LANES), (lax.axis_size("gy"), EDGE_ROWS, LANES)],
        [SMEM, HBM, HBM, HBM],
        [
            pltpu.VMEM((NREG, sweep_gain.shape[0]), jnp.float32),
            pltpu.VMEM((R * CELLS, LANES), jnp.float32),
            pltpu.VMEM((CELLS, LANES), jnp.int32),
            pltpu.SemaphoreType.DMA((3,)),
        ],
        60,
    )(sweep_index, sweep_gain.T, sources.reshape(R * CELLS, LANES), labels.reshape(CELLS, LANES))
    edges = lax.all_to_all(edge, "gy", 0, 0)
    block = call(join_kernel, "join", [(CELLS + 2, R, LANES)], [VMEM] * 2)(block, edges)[0]
    low, high = neighbour(block, "gx", 1), neighbour(block, "gx", -1)
    down, up = call(merge_kernel, "merge", [(PLANES, R, LANES)] * 2, [VMEM] * 3)(
        block, low, high
    )
    below, above = neighbour(up, "gz", 1), neighbour(down, "gz", -1)
    basis, moments = call(
        power_kernel,
        "powers",
        [(S + 1, CELLS, R, LANES), (2 * R, LANES)],
        [SMEM] + [VMEM] * 6,
        [
            pltpu.VMEM((WIDE, 2 * HALF, LANES), jnp.float32),
            pltpu.VMEM((4, WIDE, 2 * HALF, LANES), jnp.float32),
            pltpu.VMEM((7, WIDE, 2 * HALF, LANES), jnp.float32),
            pltpu.VMEM((WIDE, WIDE, 2, R, LANES), jnp.float32),
            pltpu.VMEM((WIDE, WIDE, 2, R, LANES), jnp.float32),
        ],
            24,
    )(region_table.T, block, low, high, down, below, above)
    solution, residual = call(
        solve_kernel, "solve", [(R * CELLS, LANES)] * 2, [VMEM] * 2
    )(total(moments), basis)
    return (solution.reshape(sources.shape), residual.reshape(sources.shape))


def solution(mesh):
    placed = (P(None, "gz", "gx", "gy"), P("gz", "gx", "gy"), P(), P(), P())
    return jax.shard_map(
        body,
        mesh=mesh,
        in_specs=placed,
        out_specs=(P(None, "gz", "gx", "gy"), P(None, "gz", "gx", "gy")),
        check_vma=False,
    )
```

```python
import jax
import jax.numpy as jnp
from jax import lax
from jax.experimental import pallas as pl
from jax.experimental.pallas import tpu as pltpu
from jax.sharding import PartitionSpec as P

S = 4
NREG = 8
R = 32
SIDE = 4
CELLS = SIDE * SIDE
LANES = 128
WIDE = SIDE + 2 * S
HALF = 16
EDGE_ROWS = R + 8
KEPT = sum(SIDE + 2 * (S - d) for d in range(1, S + 1))
PLANES = KEPT + 3


SIGMA = 8.0
THETA = 8.0

VMEM = pl.BlockSpec(memory_space=pltpu.VMEM)
SMEM = pl.BlockSpec(memory_space=pltpu.SMEM)
HBM = pl.BlockSpec(memory_space=pltpu.HBM)


def call(kernel, name, outs, specs, scratch=(), mebi=8):
    return pl.pallas_call(
        kernel,
        name=name,
        out_shape=[jax.ShapeDtypeStruct(shape, jnp.float32) for shape in outs],
        in_specs=specs,
        out_specs=[VMEM] * len(outs),
        scratch_shapes=list(scratch),
        compiler_params=pltpu.CompilerParams(vmem_limit_bytes=mebi * 1024 * 1024),
    )


def lane_index(shape):
    return lax.broadcasted_iota(jnp.int32, shape, len(shape) - 1)


def rhs_kernel(
    index_ref, gain_hbm, source_hbm, label_hbm, block_ref, edge_ref, gain_ref, source_ref, label_ref, sems
):
    copies = [
        pltpu.make_async_copy(gain_hbm, gain_ref, sems.at[0]),
        pltpu.make_async_copy(label_hbm, label_ref, sems.at[1]),
        pltpu.make_async_copy(source_hbm, source_ref, sems.at[2]),
    ]
    for copy in copies:
        copy.start()
    sub = lax.broadcasted_iota(jnp.int32, (R, gain_ref.shape[1]), 0)
    point = jnp.zeros(sub.shape, jnp.int32)
    for j in range(R):
        point = jnp.where(sub == j, index_ref[j], point)
    copies[0].wait()
    rows = lax.dot_general(
        (point == lane_index(point.shape)).astype(jnp.float32),
        gain_ref[...],
        (((1,), (1,)), ((), ())),
        precision=lax.Precision.HIGHEST,
        preferred_element_type=jnp.float32,
    )
    copies[1].wait()
    copies[2].wait()
    columns = [jnp.broadcast_to(rows[:, k : k + 1], (R, LANES)) for k in range(NREG)]
    group = lane_index((R, LANES)) // (2 * S)
    group_row = lane_index((8, LANES)) // (2 * S)
    edge = jnp.zeros((R, LANES), jnp.float32)
    edge_label = jnp.zeros((8, LANES), jnp.float32)
    labels = label_ref[...].astype(jnp.float32)
    for cell in range(CELLS):
        label = jnp.broadcast_to(labels[cell : cell + 1, :], (R, LANES))
        gain = jnp.zeros((R, LANES), jnp.float32)
        for k in range(NREG):
            gain = jnp.where(label == k + 1.0, columns[k], gain)
        rhs = source_ref[pl.ds(cell, R, stride=CELLS), :] * gain
        block_ref[cell] = rhs
        turn = (cell * 2 * S + S) % LANES
        edge = jnp.where(group == cell, pltpu.roll(rhs, turn, 1), edge)
        edge_label = jnp.where(
            group_row == cell, pltpu.roll(label[:8], turn, 1), edge_label
        )
    block_ref[CELLS, 0:CELLS, :] = labels
    block_ref[CELLS, CELLS:R, :] = jnp.zeros((R - CELLS, LANES), jnp.float32)
    for slot in range(edge_ref.shape[0]):
        edge_ref[slot, 0:R, :] = edge
        edge_ref[slot, R:EDGE_ROWS, :] = edge_label


def join_kernel(block_ref, edges_ref, out_ref):
    count = edges_ref.shape[0]
    place = lax.axis_index("gy")
    left = lane_index((EDGE_ROWS, LANES)) % (2 * S) < S
    before = jnp.where(place > 0, edges_ref[jnp.maximum(place - 1, 0)], 0.0)
    after = jnp.where(place < count - 1, edges_ref[jnp.minimum(place + 1, count - 1)], 0.0)
    edge = jnp.where(left, before, after)
    out_ref[0 : CELLS + 1] = block_ref[...]
    out_ref[CELLS, CELLS : CELLS + 1, :] = edge[R : R + 1]
    out_ref[CELLS + 1] = edge[:R]


def kept_cells(order):
    return [
        (row, x)
        for d, row in zip(range(1, S + 1), order)
        for x in range(-(S - d), SIDE + S - d)
    ]


def merge_kernel(own_ref, low_ref, high_ref, down_ref, up_ref):
    blocks = (low_ref, own_ref, high_ref)
    for out_ref, order in ((down_ref, (0, 1, 2, 3)), (up_ref, (3, 2, 1, 0))):
        for slot, (row, x) in enumerate(kept_cells(order)):
            out_ref[slot] = blocks[(x + SIDE) // SIDE][row * SIDE + x % SIDE]
            label = blocks[(x + SIDE) // SIDE][CELLS, row * SIDE + x % SIDE : row * SIDE + x % SIDE + 1, :]
            out_ref[KEPT + 2, slot : slot + 1, :] = label
        low_side = lane_index((R, LANES)) // (2 * S) % SIDE >= SIDE // 2
        out_ref[KEPT] = own_ref[CELLS + 1]
        out_ref[KEPT + 1] = jnp.where(low_side, low_ref[CELLS + 1], high_ref[CELLS + 1])
        for g in range(3):
            edge = blocks[g][CELLS, CELLS : CELLS + 1, :]
            out_ref[KEPT + 2, KEPT + g : KEPT + g + 1, :] = edge
        out_ref[KEPT + 2, KEPT + 3 : R, :] = jnp.zeros((R - KEPT - 3, LANES), jnp.float32)


def coefficients(table_ref, label_ref, cond_ref, coef_ref):
    def conduct(z, carry):
        label = label_ref[z]
        fields = [jnp.zeros((2 * HALF, LANES), jnp.float32) for _ in range(4)]
        for region in range(NREG):
            hit = label == region + 1.0
            fields = [
                jnp.where(hit, table_ref[column, region], fields[column]) for column in range(4)
            ]
        for column in range(4):
            cond_ref[column, z] = fields[column]
        return carry

    lax.fori_loop(0, WIDE, conduct, 0, unroll=3)
    lane = lane_index((2 * HALF, LANES))

    def faces(z, carry):
        inside = label_ref[z] > 0.5
        along_z, along_x, along_y, shunt = (cond_ref[column, z] for column in range(4))
        after = pltpu.roll(along_y, LANES - 1, 1)
        before = pltpu.roll(along_y, 1, 1)
        after = jnp.where(lane == LANES - 1, pltpu.roll(after, HALF, 0), after)
        before = jnp.where(lane == 0, pltpu.roll(before, HALF, 0), before)
        found = [
            0.5 * (along_z + cond_ref[0, z + 1]),
            0.5 * (along_z + cond_ref[0, z - 1]),
            0.5 * (along_x + pltpu.roll(along_x, 2 * HALF - 1, 0)),
            0.5 * (along_x + pltpu.roll(along_x, 1, 0)),
            0.5 * (along_y + after),
            0.5 * (along_y + before),
        ]
        diag = shunt
        for face in found:
            diag = diag + face
        found.append(diag - SIGMA)
        for k, value in enumerate(found):
            coef_ref[k, z] = jnp.where(inside, value * (1.0 / THETA), 0.0)
        return carry

    lax.fori_loop(1, WIDE - 1, faces, 0, unroll=5)


def outside(at):
    return max(0, S - at, at - (S + SIDE - 1))


def power_row(source_ref, target_ref, coef_ref, z, reach):
    lane = lane_index((R, LANES))
    first, last = lane == 0, lane == LANES - 1
    for x in range(S - reach, S + SIDE + reach):
        center = [source_ref[z, x, t] for t in range(2)]
        for t in range(1 if outside(x) == reach else 2):
            row = t * HALF + x
            here, there = center[t], center[1 - t]
            before = pltpu.roll(jnp.where(last, there, here), 1, 1)
            after = pltpu.roll(jnp.where(first, there, here), LANES - 1, 1)

            def weight(k):
                return jnp.broadcast_to(coef_ref[k, z, row : row + 1, :], (R, LANES))

            beside = weight(0) * source_ref[z + 1, x, t] + weight(1) * source_ref[z - 1, x, t]
            beside = beside + weight(2) * source_ref[z, x + 1, t]
            beside = beside + weight(3) * source_ref[z, x - 1, t]
            beside = beside + weight(4) * after + weight(5) * before
            target_ref[z, x, t] = weight(6) * here - beside


def power_kernel(
    table_ref,
    own_ref,
    low_ref,
    high_ref,
    below_ref,
    above_ref,
    basis_ref,
    moment_ref,
    label_ref,
    cond_ref,
    coef_ref,
    even_ref,
    odd_ref,
):
    blocks = (low_ref, own_ref, high_ref)
    label_ref[...] = jnp.zeros(label_ref.shape, jnp.float32)
    sides = ((0, below_ref, (3, 2, 1, 0)), (S, None, None), (S + SIDE, above_ref, (0, 1, 2, 3)))
    for base, ref, order in sides:
        if ref is not None:
            for slot, (row, x) in enumerate(kept_cells(order)):
                label_ref[base + row, S + x : S + x + 1, :] = ref[KEPT + 2, slot : slot + 1, :]
        for g in range(3):
            if ref is None:
                edge = blocks[g][CELLS, CELLS : CELLS + 1, :]
            else:
                edge = ref[KEPT + 2, KEPT + g : KEPT + g + 1, :]
            for row in range(SIDE):
                if ref is None:
                    labels = blocks[g][CELLS, row * SIDE : (row + 1) * SIDE, :]
                    label_ref[base + row, g * SIDE : (g + 1) * SIDE, :] = labels
                for x in range(SIDE):
                    if outside(base + row) + outside(g * SIDE + x) >= S:
                        continue
                    turn = -((row * SIDE + x) * 2 * S + S) % LANES
                    at = HALF + g * SIDE + x
                    label_ref[base + row, at : at + 1, :] = pltpu.roll(edge, turn, 1)
    coefficients(table_ref, label_ref, cond_ref, coef_ref)

    for row in range(SIDE):
        for x in range(-S, SIDE + S):
            even_ref[S + row, S + x, 0] = blocks[(x + SIDE) // SIDE][row * SIDE + x % SIDE]
    for slot, (row, x) in enumerate(kept_cells((3, 2, 1, 0))):
        even_ref[row, S + x, 0] = below_ref[slot]
    for slot, (row, x) in enumerate(kept_cells((0, 1, 2, 3))):
        even_ref[S + SIDE + row, S + x, 0] = above_ref[slot]
    for base, ref, _ in sides:
        for g in range(3):
            if ref is None:
                edge = blocks[g][CELLS + 1]
            else:
                edge = ref[KEPT + (g != 1)]
            for row in range(SIDE):
                for x in range(SIDE):
                    if outside(base + row) + outside(g * SIDE + x) >= S:
                        continue
                    turn = -((row * SIDE + x) * 2 * S + S) % LANES
                    even_ref[base + row, g * SIDE + x, 1] = pltpu.roll(edge, turn, 1)

    def keep(k):
        for row in range(SIDE):
            for x in range(SIDE):
                basis_ref[k, row * SIDE + x] = refs[k % 2][S + row, S + x, 0]

    def moments(k):
        this = jnp.concatenate([basis_ref[k, cell] for cell in range(CELLS)], 1)
        after = jnp.concatenate([basis_ref[k + 1, cell] for cell in range(CELLS)], 1)
        pair = lax.dot_general(
            this,
            jnp.concatenate([this, after], 0),
            (((1,), (1,)), ((), ())),
            precision=lax.Precision.HIGHEST,
            preferred_element_type=jnp.float32,
        )
        half, at = divmod(2 * k * R, LANES)
        moment_ref[half * R : (half + 1) * R, at : at + 2 * R] = pair

    refs = (even_ref, odd_ref)
    keep(0)
    for k in range(S - 1):
        now, later = refs[k % 2], refs[1 - k % 2]
        for far in range(S - k):
            reach = S - 1 - k - far

            def one(i, carry):
                for z in (S + 2 * i, S + 2 * i + 1):
                    power_row(now, later, coef_ref, z, reach)
                return carry

            if far == 0:
                lax.fori_loop(0, SIDE // 2, one, 0)
            else:
                for z in (S - far, S + SIDE - 1 + far):
                    power_row(now, later, coef_ref, z, reach)
        keep(k + 1)
    for k in range(S - 1):
        moments(k)
    for row in range(SIDE):
        power_row(refs[(S - 1) % 2], refs[S % 2], coef_ref, S + row, 0)
    keep(S)
    moments(S - 1)


def eliminate(mat, right):
    for g in range(S):
        rows = slice(g * R, (g + 1) * R)
        solved, sides = eliminate_rows(mat[rows], right[rows], g * R)
        both = jnp.concatenate([solved, sides], 1)
        taken = jnp.dot(
            mat[:, rows],
            both,
            precision=lax.Precision.HIGHEST,
            preferred_element_type=jnp.float32,
        )
        parts = []
        for h in range(S):
            at = slice(h * R, (h + 1) * R)
            parts.append(
                (solved, sides)
                if h == g
                else (mat[at] - taken[at, :LANES], right[at] - taken[at, LANES:])
            )
        mat = jnp.concatenate([part[0] for part in parts], 0)
        right = jnp.concatenate([part[1] for part in parts], 0)
    return right


def eliminate_rows(mat, right, begin):
    count = R // 8
    tiles = [mat[8 * i : 8 * i + 8] for i in range(count)]
    sides = [right[8 * i : 8 * i + 8] for i in range(count)]
    sub = lax.broadcasted_iota(jnp.int32, (8, LANES), 0)

    def spread(row):
        return jnp.broadcast_to(row, (8, LANES))

    for p in range(count):
        k = begin + 8 * p
        a = [spread(tiles[p][i : i + 1, :]) for i in range(8)]
        b = [spread(sides[p][i : i + 1, :]) for i in range(8)]
        e = {(i, j): spread(a[i][:, k + j : k + j + 1]) for i in range(8) for j in range(i, 8)}
        upper = {}
        for m in range(0, 8, 2):
            n = m + 1
            inv = 1.0 / (e[m, m] * e[n, n] - e[m, n] * e[m, n])
            q00, q01, q11 = e[n, n] * inv, -e[m, n] * inv, e[m, m] * inv
            for j in range(m + 2, 8):
                upper[m, j] = q00 * e[m, j] + q01 * e[n, j]
                upper[n, j] = q01 * e[m, j] + q11 * e[n, j]
            for i in range(m + 2, 8):
                for j in range(i, 8):
                    e[i, j] = e[i, j] - (e[m, i] * upper[m, j] + e[n, i] * upper[n, j])
            for rows in (a, b):
                for j in range(m + 2, 8):
                    rows[j] = rows[j] - (upper[m, j] * rows[m] + upper[n, j] * rows[n])
                rows[m], rows[n] = q00 * rows[m] + q01 * rows[n], q01 * rows[m] + q11 * rows[n]
        for rows in (a, b):
            for m in range(6, 0, -2):
                for i in range(m):
                    rows[i] = rows[i] - (upper[i, m] * rows[m] + upper[i, m + 1] * rows[m + 1])
        for i in range(count):
            if i == p:
                continue
            col = [spread(tiles[i][:, k + j : k + j + 1]) for j in range(8)]
            for parts, rows in ((tiles, a), (sides, b)):
                terms = [col[j] * rows[j] for j in range(8)]
                pairs = [terms[j] + terms[j + 1] for j in range(0, 8, 2)]
                parts[i] = parts[i] - ((pairs[0] + pairs[1]) + (pairs[2] + pairs[3]))
        for parts, rows in ((tiles, a), (sides, b)):
            merged = rows[0]
            for j in range(1, 8):
                merged = jnp.where(sub == j, rows[j], merged)
            parts[p] = merged
    return jnp.concatenate(tiles, 0), jnp.concatenate(sides, 0)


def solve_kernel(moment_ref, basis_ref, solution_ref, residual_ref):
    low, high = moment_ref[0:R, :], moment_ref[R : 2 * R, :]
    lane = lane_index((R, LANES))

    def window(first, second, shift):
        if shift == 0:
            return first
        keep = lane < LANES - shift
        turn = LANES - shift
        return jnp.where(keep, pltpu.roll(first, turn, 1), pltpu.roll(second, turn, 1))

    first = THETA * window(low, high, R) + SIGMA * low
    second = THETA * window(high, high, R) + SIGMA * high
    mat = jnp.concatenate([window(first, second, i * R) for i in range(S)], 0)
    mat = 0.5 * (mat + mat.T)
    right = jnp.concatenate([window(low, high, i * R) for i in range(S)], 0)
    coef = eliminate(mat, right)
    zero = jnp.zeros((R, LANES), jnp.float32)
    here = jnp.concatenate([coef, zero], 0)
    there = jnp.concatenate([zero, coef], 0)
    combo = SIGMA * here + THETA * there
    wide = lane_index(here.shape)
    weights = jnp.where(
        wide < R, here, jnp.where(wide < 2 * R, pltpu.roll(combo, R, 1), 0.0)
    )
    weights = jnp.concatenate([weights, jnp.zeros((96, LANES), jnp.float32)], 0)
    weights = weights.T[: 2 * R, : (S + 1) * R]
    for cell in range(CELLS):
        block = jnp.concatenate([basis_ref[k, cell] for k in range(S + 1)], 0)
        taken = lax.dot_general(
            weights,
            block,
            (((1,), (0,)), ((), ())),
            precision=lax.Precision.HIGHEST,
            preferred_element_type=jnp.float32,
        )
        solution_ref[pl.ds(cell, R, stride=CELLS), :] = taken[:R]
        residual_ref[pl.ds(cell, R, stride=CELLS), :] = basis_ref[0, cell] - taken[R:]


def neighbour(value, axis, offset):
    count = lax.axis_size(axis)
    pairs = [(at, at + offset) for at in range(count) if 0 <= at + offset < count]
    return lax.ppermute(value, axis, pairs)


def total(values):
    near = ("gy", "gz")
    parts = lax.axis_size("gy") * lax.axis_size("gz")
    others = lax.axis_size("gx")
    piece = lax.all_to_all(values.reshape(parts, -1, LANES), near, 0, 0).sum(0)
    pieces = lax.all_to_all(jnp.broadcast_to(piece, (others,) + piece.shape), "gx", 0, 0)
    piece = pieces.sum(0)
    pieces = lax.all_to_all(jnp.broadcast_to(piece, (parts,) + piece.shape), near, 0, 0)
    return pieces.reshape(values.shape)


def body(sources, labels, region_table, sweep_index, sweep_gain):
    block, edge = call(
        rhs_kernel,
        "rhs",
        [(CELLS + 1, R, LANES), (lax.axis_size("gy"), EDGE_ROWS, LANES)],
        [SMEM, HBM, HBM, HBM],
        [
            pltpu.VMEM((NREG, sweep_gain.shape[0]), jnp.float32),
            pltpu.VMEM((R * CELLS, LANES), jnp.float32),
            pltpu.VMEM((CELLS, LANES), jnp.int32),
            pltpu.SemaphoreType.DMA((3,)),
        ],
        60,
    )(sweep_index, sweep_gain.T, sources.reshape(R * CELLS, LANES), labels.reshape(CELLS, LANES))
    edges = lax.all_to_all(edge, "gy", 0, 0)
    block = call(join_kernel, "join", [(CELLS + 2, R, LANES)], [VMEM] * 2)(block, edges)[0]
    low, high = neighbour(block, "gx", 1), neighbour(block, "gx", -1)
    down, up = call(merge_kernel, "merge", [(PLANES, R, LANES)] * 2, [VMEM] * 3)(
        block, low, high
    )
    below, above = neighbour(up, "gz", 1), neighbour(down, "gz", -1)
    basis, moments = call(
        power_kernel,
        "powers",
        [(S + 1, CELLS, R, LANES), (2 * R, LANES)],
        [SMEM] + [VMEM] * 5,
        [
            pltpu.VMEM((WIDE, 2 * HALF, LANES), jnp.float32),
            pltpu.VMEM((4, WIDE, 2 * HALF, LANES), jnp.float32),
            pltpu.VMEM((7, WIDE, 2 * HALF, LANES), jnp.float32),
            pltpu.VMEM((WIDE, WIDE, 2, R, LANES), jnp.float32),
            pltpu.VMEM((WIDE, WIDE, 2, R, LANES), jnp.float32),
        ],
            24,
    )(region_table.T, block, low, high, below, above)
    solution, residual = call(
        solve_kernel, "solve", [(R * CELLS, LANES)] * 2, [VMEM] * 2
    )(total(moments), basis)
    return (solution.reshape(sources.shape), residual.reshape(sources.shape))


def solution(mesh):
    placed = (P(None, "gz", "gx", "gy"), P("gz", "gx", "gy"), P(), P(), P())
    return jax.shard_map(
        body,
        mesh=mesh,
        in_specs=placed,
        out_specs=(P(None, "gz", "gx", "gy"), P(None, "gz", "gx", "gy")),
        check_vma=False,
    )
```
